128 devices in a mesh: dp: 16 (over y_lo, z, core), tensor: 8 (over x, y_hi).
Axes of the slice: x: 4, y: 4 (y_hi: 2, y_lo: 2; y = y_hi * 2 + y_lo), z: 4, core: 2. Of those that a mesh axis runs over, the one named last changes fastest.
Arguments:
- teacher_context: bfloat16 [20480, 8192], P('dp', 'tensor'), may hold values from -6 to 6
- teacher_out_weight: bfloat16 [8192, 4096], P('tensor'), may hold values from -0.0625 to 0.0625
- teacher_resid: bfloat16 [20480, 4096], P(('dp', 'tensor')), may hold values from -360 to 360
- teacher_gain: float32 [4096], replicated, may hold values from 0.1 to 1.9
- projector: bfloat16 [4096, 2048], P('tensor'), may hold values from -0.09375 to 0.09375
- student_context: bfloat16 [20480, 2048], P(('dp', 'tensor')), may hold values from -24 to 24
- student_resid: bfloat16 [20480, 2048], P(('dp', 'tensor')), may hold values from -6 to 6
- student_weight: bfloat16 [2048, 2048], P(('dp', 'tensor')), may hold values from -0.125 to 0.125
Outputs:
- weight_grad: float32 [2048, 2048], P(('dp', 'tensor'))
The draws below stay inside these ranges and needn't reach their ends.
All inputs are finite; a program needn't handle non-finite values.
Results may differ from the reference program's by a relative error of at most 0.012.
Values may be sent and summed in bfloat16 or wider, within the bound.
A program may use at most 128 MiB of HBM per device.

```python
import jax
import jax.numpy as jnp
from jax import lax

TH = 8192
TD = 4096
SI = 2048
SD = 2048
TOKENS = 20480
N_TENSOR = 8


def draw_teacher_resid(key, part):
    key = jax.random.fold_in(key, 11)
    key_rows, key_cols, key_base = jax.random.split(key, 3)
    row_scale = jnp.exp(jnp.log(10.0) * jax.random.uniform(key_rows, (TOKENS, 1), jnp.float32))
    rising = jnp.exp(jnp.log(3.0) * jnp.arange(TD, dtype=jnp.float32) / TD)
    col_scale = jnp.exp(jnp.log(10.0) * jax.random.uniform(key_cols, (1, TD), jnp.float32)) * rising[None, :]
    base = jnp.clip(jax.random.normal(key_base, (TOKENS, TD), jnp.float32), -4.0, 4.0)
    return (0.3 * row_scale * col_scale * base).astype(jnp.bfloat16)


def strengthened(values, stream_key, source, target, shards_of, factor):
    def block_of(position):
        return (jnp.arange(values.shape[position]) // (values.shape[position] // shards_of)).reshape((-1,) + (1,) * (values.ndim - 1 - position))

    first = jax.random.permutation(stream_key, shards_of)[block_of(target)]
    second = (block_of(target) + shards_of // 2) % shards_of
    return jnp.where((block_of(source) == first) | (block_of(source) == second), factor * values, values)


def steps_of(key, dims, cuts, smallest, largest):
    level = 1.0
    for axis_at, shards_of in cuts:
        steps = jax.random.uniform(jax.random.fold_in(jax.random.fold_in(key, 6), axis_at), (shards_of,), jnp.float32, smallest / len(cuts), largest / len(cuts))
        level = level * jnp.repeat(jnp.exp(steps), dims[axis_at] // shards_of).reshape((-1,) + (1,) * (len(dims) - 1 - axis_at))
    return level


def normal_values(own_key, shape, scale, most, shards=(), kind=jnp.bfloat16):
    gain = steps_of(own_key, shape, shards, -0.22, 0.18) if shards else 1.0
    drawn = jax.random.normal(own_key, shape, jnp.float32) * scale * gain
    return jnp.minimum(jnp.maximum(drawn, -most), most).astype(kind)


def noise_with(stream_key, extent, scale, reach, cuts, heavy, kind=jnp.bfloat16):
    values = scale * jax.random.normal(stream_key, extent, jnp.float32)
    if cuts:
        values = values * steps_of(stream_key, extent, cuts, -0.22, 0.18)
    return jnp.clip(strengthened(values, jax.random.fold_in(stream_key, 3), *heavy), -reach, reach).astype(kind)


def setup_inputs(seed: int = 0) -> dict:
    arg_keys = jax.random.split(jax.random.key(seed), 9)
    teacher_context = noise_with(arg_keys[0], (TOKENS, TH), 1.0, 6.0, ((0, 16), (1, 8)), (1, 0, 16, 2.0))
    teacher_out_weight = normal_values(arg_keys[1], (TH, TD), TH ** -0.5, 0.0625, ((0, 8),))
    teacher_resid = draw_teacher_resid(jax.random.fold_in(arg_keys[8], 71), 0)
    teacher_gain = jnp.clip(1.0 + 0.18 * jax.random.normal(arg_keys[3], (TD,), jnp.float32), 0.1, 1.9)
    projector = normal_values(arg_keys[4], (TD, SD), TD ** -0.5, 0.09375, ((0, 8),))
    student_context = noise_with(arg_keys[5], (TOKENS, SI), 1.0, 24.0, ((0, 128),), (0, 1, 128, 5.5))
    student_resid = normal_values(arg_keys[6], (TOKENS, SD), 1.0, 6.0, ((0, 128),))
    student_weight = normal_values(arg_keys[7], (SI, SD), SI ** -0.5, 0.125, ((0, 128),))
    return {"teacher_context": teacher_context, "teacher_out_weight": teacher_out_weight, "teacher_resid": teacher_resid, "teacher_gain": teacher_gain, "projector": projector, "student_context": student_context, "student_resid": student_resid, "student_weight": student_weight}


def blocked_product(left, right, pieces):
    span_width = left.shape[1] // pieces
    result = jnp.zeros((left.shape[0], right.shape[1]), jnp.float32)
    for block_index in range(pieces):
        partial_sum = jnp.dot(left[:, block_index * span_width:(block_index + 1) * span_width], right[block_index * span_width:(block_index + 1) * span_width], preferred_element_type=jnp.float32)
        result = result + lax.optimization_barrier(partial_sum.astype(jnp.bfloat16)).astype(jnp.float32)
    return result

def reference(teacher_context, teacher_out_weight, teacher_resid, teacher_gain, projector, student_context, student_resid, student_weight):
    attended = blocked_product(teacher_context, teacher_out_weight, N_TENSOR)
    hidden = teacher_resid.astype(jnp.float32) + attended
    inverse = lax.rsqrt(lax.optimization_barrier(jnp.mean(hidden * hidden, axis=-1, keepdims=True)) + 1e-05)
    normed = (hidden * inverse * teacher_gain.astype(jnp.float32)).astype(jnp.bfloat16)
    target = blocked_product(normed, projector, N_TENSOR)
    student_out = student_resid.astype(jnp.float32) + jnp.dot(student_context, student_weight, preferred_element_type=jnp.float32)
    out_grad = (128.0 / TOKENS * (student_out - target)).astype(jnp.bfloat16)
    return jnp.dot(student_context.T, out_grad, preferred_element_type=jnp.float32)
```

```python
import jax
import jax.numpy as jnp
from jax import lax
from jax.experimental import pallas as pl
from jax.experimental.pallas import tpu as pltpu
from jax.sharding import PartitionSpec as P

MESH = pl.DeviceIdType.MESH
BF16 = jnp.bfloat16
F32 = jnp.float32

GATHER_PARTS = ((0, 768, "y"), (768, 256, "z"))
GRAD_PARTS = ((0, 384, "xyz"), (384, 384, "yzx"), (768, 256, "zxy"))
N_SEM = 176
N_LOCAL = 20
CHUNKS = 4


def step(v, by):
    return lax.rem(v + by, 4)


class Net:
    def __init__(self, send_sems, recv_sems, local_sems):
        dp, t = lax.axis_index("dp"), lax.axis_index("tensor")
        self.x = lax.div(t, 2)
        self.y = lax.rem(t, 2) * 2 + lax.div(dp, 8)
        self.z = lax.rem(lax.div(dp, 2), 4)
        self.c = lax.rem(dp, 2)
        self.send_sems, self.recv_sems, self.local_sems = send_sems, recv_sems, local_sems
        self.used = self.used_local = 0
        self.sent = []

    def at(self, x=0, y=0, z=0, c=0):
        px, py, pz = step(self.x, x), step(self.y, y), step(self.z, z)
        pc = lax.rem(self.c + c, 2)
        return (lax.rem(py, 2) * 8 + pz * 2 + pc, px * 2 + lax.div(py, 2))

    def send(self, src, dst, **where):
        i = self.used
        self.used += 1
        copy = pltpu.make_async_remote_copy(
            src_ref=src,
            dst_ref=dst,
            send_sem=self.send_sems.at[i],
            recv_sem=self.recv_sems.at[i],
            device_id=self.at(**where),
            device_id_type=MESH,
        )
        copy.start()
        self.sent.append(copy)
        return copy

    def load(self, src, dst):
        i = self.used_local
        self.used_local += 1
        copy = pltpu.make_async_copy(src, dst, self.local_sems.at[i])
        copy.start()
        return copy


def kernel(
    a_in, w_in, r_in, gain, p_in, s_in, sr_in, ws_in, out,
    a_v, w_v, c_v, ra, rb, ry, h_v, r_v, n_v, p_v, ws_v, s_v, sr_v, so_v, g_v, grad, o_recv, o_send,
    rg00, rg01, rg02, rg10, rg11, rg12, rg20, rg21, rg22,
    send_sems, recv_sems, local_sems,
):
    rg = ((rg00, rg01, rg02), (rg10, rg11, rg12), (rg20, rg21, rg22))
    net = Net(send_sems, recv_sems, local_sems)
    x, y, z, c = net.x, net.y, net.z, net.c
    other_c = 1 - c
    yh, yl = lax.div(y, 2), lax.rem(y, 2)
    other_yh = 1 - yh
    mine = pl.ds(pl.multiple_of(c * 1024, 1024), 1024)
    theirs = pl.ds(pl.multiple_of(other_c * 1024, 1024), 1024)

    load_a = net.load(a_in, a_v)
    w_loads = {}

    def load_w(n):
        k = n % CHUNKS
        w_loads[n] = net.load(w_in.at[:, pl.ds(k * 1024, 1024)], w_v.at[n % 2])

    load_w(0)
    load_w(1)
    early = [
        net.load(p_in.at[yl, z, :, mine], p_v.at[x, yh, yl, z]),
        net.load(ws_in.at[:, mine], ws_v.at[yl, z, c, x, yh]),
        net.load(s_in, s_v.at[c]),
        net.load(sr_in.at[:, mine], sr_v.at[c]),
        net.load(r_in, r_v),
    ]

    partners = [dict(c=1)] + [{axis: by} for axis in "xyz" for by in (1, 2, 3)]
    barrier = pltpu.get_barrier_semaphore()
    for where in partners:
        pl.semaphore_signal(barrier, inc=1, device_id=net.at(**where), device_id_type=MESH)
    pl.semaphore_wait(barrier, len(partners))

    ws_pair = net.send(ws_in.at[:, theirs], ws_v.at[yl, z, c, x, yh], c=1)
    p_x = [net.send(p_in.at[yl, z, :, mine], p_v.at[x, yh, yl, z], x=by) for by in (1, 3, 2)]
    s_pair = net.send(s_in, s_v.at[c], c=1)
    sr_pair = net.send(sr_in.at[:, theirs], sr_v.at[c], c=1)

    def product(rel, k, slot):
        rows = step(x, rel)

        @pl.loop(0, 4)
        def _(j):
            cols = pl.ds(pl.multiple_of(j * 256, 256), 256)
            res = jnp.dot(a_v[rows], w_v[slot, :, cols], preferred_element_type=F32).astype(BF16)
            c_v[rel, k, 0, :, cols] = res[:160]
            c_v[rel, k, 1, :, cols] = res[160:]

    far = {}
    direct = {}
    relayed = {}
    ysent = {}

    def far_products():
        load_a.wait()
        for k in range(CHUNKS):
            w_loads[k].wait()
            product(2, k, k % 2)
            far[k] = (
                net.send(c_v.at[2, k, 0], ra.at[0, k], x=1),
                net.send(c_v.at[2, k, 1], ra.at[1, k], x=3),
            )
            load_w(k + 2)

    def near_products(k):
        n = CHUNKS + k
        w_loads[n].wait()
        product(1, k, n % 2)
        one = net.send(c_v.at[1, k, 1], rb.at[0, 1, k], x=1)
        product(3, k, n % 2)
        direct[k] = (one, net.send(c_v.at[3, k, 0], rb.at[1, 0, k], x=3))

    def relay(k):
        far[k][0].wait_recv()
        c_v[1, k, 0] = (c_v[1, k, 0].astype(F32) + ra[0, k].astype(F32)).astype(BF16)
        one = net.send(c_v.at[1, k, 0], rb.at[0, 0, k], x=1)
        far[k][1].wait_recv()
        c_v[3, k, 1] = (c_v[3, k, 1].astype(F32) + ra[1, k].astype(F32)).astype(BF16)
        relayed[k] = (one, net.send(c_v.at[3, k, 1], rb.at[1, 1, k], x=3))
        n = CHUNKS + k
        product(0, k, n % 2)
        if n + 2 < 2 * CHUNKS:
            load_w(n + 2)

    def x_sum(k):
        for copy in direct[k] + relayed[k]:
            copy.wait_recv()

        def total(h):
            return c_v[0, k, h].astype(F32) + rb[0, h, k].astype(F32) + rb[1, h, k].astype(F32)

        c_v[0, k, other_yh] = total(other_yh).astype(BF16)
        ysent[k] = net.send(c_v.at[0, k, other_yh], ry.at[k], y=2)
        cols = pl.ds(k * 1024, 1024)
        h_v[:, cols] = total(yh) + r_v[:, cols].astype(F32)

    squares = []

    def y_sum(k):
        ysent[k].wait_recv()
        cols = pl.ds(k * 1024, 1024)
        hidden = h_v[:, cols] + ry[k].astype(F32)
        h_v[:, cols] = hidden
        squares.append(jnp.sum(hidden * hidden, axis=-1, keepdims=True))

    def piece(yv, zv, start, width):
        h, l, cols = lax.div(yv, 2), lax.rem(yv, 2), pl.ds(start, width)
        return p_v.at[:, h, l, zv, :, cols], ws_v.at[l, zv, :, :, h, :, cols]

    gathers = {}

    def gather_send(key, yv, zv, start, width, axis, by):
        gathers[key] = [net.send(ref, ref, **{axis: by}) for ref in piece(yv, zv, start, width)]

    def gather_wait(*key):
        for copy in gathers[key]:
            copy.wait_recv()

    place = {"y": y, "z": z}

    def ring(part, axis, item):
        start, width, _ = GATHER_PARTS[part]
        yz = (y, step(z, item)) if axis == "y" else (step(y, item), z)
        for by in (1, 3):
            gather_send((part, axis, item, by), *yz, start, width, axis, by)

    def onward(part, axis, item):
        start, width, _ = GATHER_PARTS[part]
        half = width // 2
        for by, begin in ((1, start), (3, start + half)):
            gather_wait(part, axis, item, by)
            source = step(place[axis], 4 - by)
            yz = (source, step(z, item)) if axis == "y" else (step(y, item), source)
            gather_send((part, axis, item, by, "on"), *yz, begin, half, axis, by)

    def arrived(part, axis, item):
        for by in (1, 3):
            gather_wait(part, axis, item, by, "on")

    def gather_x():
        for copy in early[:2]:
            copy.wait()
        ws_pair.wait_recv()
        ref = ws_v.at[yl, z, :, x, yh]
        return [net.send(ref, ref, x=by) for by in (1, 3, 2)]

    def gather_begin(ws_x):
        for copy in p_x + ws_x:
            copy.wait_recv()
        ring(1, "z", 0)
        ring(0, "y", 0)
        ring(0, "z", 0)
        ring(1, "y", 0)

    ws_x = gather_x()
    far_products()
    gather_begin(ws_x)
    near_products(0)
    relay(0)
    onward(1, "z", 0)
    near_products(1)
    relay(1)
    onward(0, "y", 0)
    ring(0, "z", 3)
    ring(0, "z", 1)
    onward(0, "z", 0)
    ring(1, "y", 3)
    ring(1, "y", 1)
    near_products(2)
    relay(2)
    arrived(1, "z", 0)
    ring(1, "y", 2)
    onward(1, "y", 0)
    arrived(0, "y", 0)
    ring(0, "z", 2)
    near_products(3)
    relay(3)
    for copy in early[2:]:
        copy.wait()
    onward(1, "y", 3)
    onward(1, "y", 1)
    onward(0, "z", 3)
    x_sum(0)
    onward(1, "y", 2)
    onward(0, "z", 1)
    y_sum(0)
    x_sum(1)
    y_sum(1)
    onward(0, "z", 2)
    x_sum(2)
    y_sum(2)
    s_pair.wait_recv()
    sr_pair.wait_recv()
    for item in range(4):
        arrived(0, "z", item)
        arrived(1, "y", item)

    @pl.loop(0, 4)
    def _(j):
        cols = pl.ds(pl.multiple_of(j * 256, 256), 256)
        so_v[:, cols] = sr_v[:, :, cols].reshape(320, 256).astype(F32) + jnp.dot(
            s_v[...].reshape(320, 2048),
            ws_v[:, :, :, :, :, :, cols].reshape(2048, 256),
            preferred_element_type=F32,
        )

    x_sum(3)
    y_sum(3)

    inverse = lax.rsqrt(sum(squares) * (1.0 / 4096.0) + 1e-05)
    n_pair = []
    for k in range(CHUNKS):
        cols = pl.ds(k * 1024, 1024)
        n_v[c, :, cols] = (h_v[:, cols] * inverse * gain[:, cols]).astype(BF16)
        n_pair.append(net.send(n_v.at[c, :, cols], n_v.at[c, :, cols], c=1))
    for k in range(CHUNKS):
        n_pair[k].wait_recv()

        @pl.loop(0, 4)
        def _(j):
            cols = pl.ds(pl.multiple_of(j * 256, 256), 256)
            so_v[:, cols] -= jnp.dot(
                n_v[:, :, pl.ds(k * 1024, 1024)].reshape(320, 1024),
                p_v[k, :, :, :, :, cols].reshape(1024, 256),
                preferred_element_type=F32,
            )

    g_v[...] = (128.0 / 20480.0 * so_v[...]).astype(BF16)

    def grad_piece(yv, zv, xv, cols):
        every = slice(None)
        l, h = (every, every) if yv is None else (lax.rem(yv, 2), lax.div(yv, 2))
        return (l, every if zv is None else zv, every, every if xv is None else xv, h, every, cols)

    where = {"x": x, "y": y, "z": z}
    fixed = [dict(x=None, y=None, z=None) for _ in GRAD_PARTS]
    grads = {}

    def grad_send(part, stage):
        start, width, order = GRAD_PARTS[part]
        axis = order[stage]
        cols = pl.ds(start, width)
        for rel in (1, 3, 2):
            to = dict(fixed[part])
            to[axis] = step(where[axis], rel)
            ref = grad.at[grad_piece(to["y"], to["z"], to["x"], cols)]
            grads[part, stage, rel] = net.send(ref, rg[part][stage].at[rel - 1], **{axis: rel})
        fixed[part][axis] = where[axis]

    def grad_sum(part, stage):
        start, width, order = GRAD_PARTS[part]
        for rel in (1, 3, 2):
            grads[part, stage, rel].wait_recv()
        own = grad_piece(fixed[part]["y"], fixed[part]["z"], fixed[part]["x"], pl.ds(start, width))
        total = grad[own].astype(F32)
        for i in range(3):
            total = total + rg[part][stage][i].astype(F32)
        return own, total

    for part, (start, width, order) in enumerate(GRAD_PARTS):
        cols = pl.ds(start, width)

        @pl.loop(0, 8)
        def _(i):
            rows = pl.ds(pl.multiple_of(i * 256, 256), 256)
            res = lax.dot_general(
                s_v[:, :, rows].reshape(320, 256),
                g_v[:, cols],
                (((0,), (0,)), ((), ())),
                preferred_element_type=F32,
            )
            grad[lax.div(i, 4), lax.rem(i, 4), :, :, :, :, cols] = res.astype(BF16).reshape(2, 4, 2, 16, width)

        grad_send(part, 0)

    for stage in range(2):
        for part in range(3):
            own, total = grad_sum(part, stage)
            grad[own] = total.astype(BF16)
            grad_send(part, stage + 1)

    last = []
    for part, (start, width, _) in enumerate(GRAD_PARTS):
        _, total = grad_sum(part, 2)
        cols = pl.ds(start, width)
        o_send[:, :, cols] = total
        ref = o_send.at[other_c, :, cols]
        last.append(net.send(ref, o_recv.at[:, cols], c=1))
    for copy in last:
        copy.wait_recv()
    out[:, mine] = o_send[c]
    out[:, theirs] = o_recv[...]

    for copy in net.sent:
        copy.wait_send()


def grad_scratch():
    shapes = []
    for _, width, order in GRAD_PARTS:
        done = set()
        for axis in order:
            done.add(axis)
            dims = [] if "y" in done else [2]
            dims += [] if "z" in done else [4]
            dims += [2]
            dims += [] if "x" in done else [4]
            dims += [] if "y" in done else [2]
            shapes.append(pltpu.VMEM((3, *dims, 16, width), BF16))
    return shapes


def per_device(a, w, resid, gain, projector, s, s_resid, ws):
    anywhere = pl.BlockSpec(memory_space=pl.ANY)
    vmem = pl.BlockSpec(memory_space=pltpu.VMEM)
    return pl.pallas_call(
        kernel,
        out_shape=jax.ShapeDtypeStruct((16, 2048), F32),
        in_specs=[anywhere, anywhere, anywhere, vmem, anywhere, anywhere, anywhere, anywhere],
        out_specs=vmem,
        scratch_shapes=[
            pltpu.VMEM((4, 320, 1024), BF16),
            pltpu.VMEM((2, 1024, 1024), BF16),
            pltpu.VMEM((4, CHUNKS, 2, 160, 1024), BF16),
            pltpu.VMEM((2, CHUNKS, 160, 1024), BF16),
            pltpu.VMEM((2, 2, CHUNKS, 160, 1024), BF16),
            pltpu.VMEM((CHUNKS, 160, 1024), BF16),
            pltpu.VMEM((160, 4096), F32),
            pltpu.VMEM((160, 4096), BF16),
            pltpu.VMEM((2, 160, 4096), BF16),
            pltpu.VMEM((4, 2, 2, 4, 64, 1024), BF16),
            pltpu.VMEM((2, 4, 2, 4, 2, 16, 1024), BF16),
            pltpu.VMEM((2, 160, 2048), BF16),
            pltpu.VMEM((2, 160, 1024), BF16),
            pltpu.VMEM((320, 1024), F32),
            pltpu.VMEM((320, 1024), BF16),
            pltpu.VMEM((2, 4, 2, 4, 2, 16, 1024), BF16),
            pltpu.VMEM((16, 1024), F32),
            pltpu.VMEM((2, 16, 1024), F32),
            *grad_scratch(),
            pltpu.SemaphoreType.DMA((N_SEM,)),
            pltpu.SemaphoreType.DMA((N_SEM,)),
            pltpu.SemaphoreType.DMA((N_LOCAL,)),
        ],
        compiler_params=pltpu.CompilerParams(
            collective_id=0, has_side_effects=True, vmem_limit_bytes=62 * 2**20
        ),
        cost_estimate=pl.CostEstimate(flops=16 * 10**9, bytes_accessed=16 * 10**6, transcendentals=160),
    )(
        a.reshape(4, 320, 1024),
        w,
        resid,
        gain.reshape(1, 4096),
        projector.reshape(2, 4, 64, 2048),
        s,
        s_resid,
        ws,
    )


def solution(mesh):
    return jax.shard_map(
        per_device,
        mesh=mesh,
        in_specs=(
            P("dp", "tensor"),
            P("tensor", None),
            P(("dp", "tensor"), None),
            P(),
            P("tensor", None),
            P(("dp", "tensor"), None),
            P(("dp", "tensor"), None),
            P(("dp", "tensor"), None),
        ),
        out_specs=P(("dp", "tensor"), None),
        check_vma=False,
    )
```

```python
import jax
import jax.numpy as jnp
from jax import lax
from jax.experimental import pallas as pl
from jax.experimental.pallas import tpu as pltpu
from jax.sharding import PartitionSpec as P

MESH = pl.DeviceIdType.MESH
BF16 = jnp.bfloat16
F32 = jnp.float32

WIDE = 512
Y_FIRST = (3, 7)
W_ORDER = (2, 3, 6, 7, 1, 0, 4, 5)
N_SEM = 179
N_LOCAL = 16


def step(v, by):
    return lax.rem(v + by, 4)


class Net:
    def __init__(self, send_sems, recv_sems, local_sems):
        dp, t = lax.axis_index("dp"), lax.axis_index("tensor")
        self.x = lax.div(t, 2)
        self.y = lax.rem(t, 2) * 2 + lax.div(dp, 8)
        self.z = lax.rem(lax.div(dp, 2), 4)
        self.c = lax.rem(dp, 2)
        self.send_sems, self.recv_sems, self.local_sems = send_sems, recv_sems, local_sems
        self.used = self.used_local = 0
        self.sent = []

    def at(self, x=0, y=0, z=0, c=0):
        px, py, pz = step(self.x, x), step(self.y, y), step(self.z, z)
        pc = lax.rem(self.c + c, 2)
        return (lax.rem(py, 2) * 8 + pz * 2 + pc, px * 2 + lax.div(py, 2))

    def send(self, src, dst, **where):
        i = self.used
        self.used += 1
        copy = pltpu.make_async_remote_copy(
            src_ref=src,
            dst_ref=dst,
            send_sem=self.send_sems.at[i],
            recv_sem=self.recv_sems.at[i],
            device_id=self.at(**where),
            device_id_type=MESH,
        )
        copy.start()
        self.sent.append(copy)
        return copy

    def load(self, src, dst):
        i = self.used_local
        self.used_local += 1
        copy = pltpu.make_async_copy(src, dst, self.local_sems.at[i])
        copy.start()
        return copy


def kernel(
    a_in, w_in, r_in, gain, p_in, s_in, sr_in, ws_in, out,
    a_v, w_v, c_v, ra, rb, ry, ry4, r_v, hg_v, p_v, ws_t, ws_v, s_v, st_v, sr_t, sr_v, t_v, so_v, g_v,
    iv_v, grad, ga1, gb1, ga2, gb2, ra2, rb2, fin, o_r,
    send_sems, recv_sems, local_sems,
):
    net = Net(send_sems, recv_sems, local_sems)
    x, y, z, c = net.x, net.y, net.z, net.c
    other_c = 1 - c
    yh, yl = lax.div(y, 2), lax.rem(y, 2)
    other_yh = 1 - yh
    my_cols = pl.ds(pl.multiple_of(z * 512 + c * 256, 256), 256)
    mine = pl.ds(pl.multiple_of(c * 256, 256), 256)
    theirs = pl.ds(pl.multiple_of(other_c * 256, 256), 256)

    def slab(zv):
        return pl.ds(pl.multiple_of(zv * 512, 512), 512)

    load_a = net.load(a_in, a_v)
    w_loads = {}

    def load_w(n):
        if n < len(W_ORDER):
            w_loads[n] = net.load(w_in.at[:, pl.ds(W_ORDER[n] * WIDE, WIDE)], w_v.at[n % 2])

    load_w(0)
    load_w(1)
    load_p = net.load(p_in.at[yl, :, my_cols], p_v.at[x, yh, yl])
    load_ws = net.load(ws_in.at[:, slab(z)], ws_t.at[z])
    load_sr = net.load(sr_in.at[:, slab(z)], sr_t.at[z])
    load_s = net.load(s_in, s_v.at[z, c])
    load_r = net.load(r_in, r_v)

    partners = [dict(c=1)] + [{axis: by} for axis in "xyz" for by in (1, 2, 3)] + [dict(z=by, c=1) for by in (1, 2, 3)]
    barrier = pltpu.get_barrier_semaphore()
    for where in partners:
        pl.semaphore_signal(barrier, inc=1, device_id=net.at(**where), device_id_type=MESH)

    def ahead(by):
        return step(x, by)

    def products(k):
        n = W_ORDER.index(k)
        w_loads[n].wait()

        @pl.loop(0, WIDE // 256)
        def _(j):
            cols = pl.ds(pl.multiple_of(j * 256, 256), 256)
            res = jnp.dot(a_v[...].reshape(1280, 1024), w_v[n % 2, :, cols], preferred_element_type=F32)
            c_v[k, :, :, :, cols] = res.astype(BF16).reshape(4, 2, 160, 256)

        load_w(n + 2)

    far, direct, relayed, ysent = {}, {}, {}, {}

    def x_far(k):
        far[k] = (
            net.send(c_v.at[k, ahead(2), 0], ra.at[k, 0], x=1),
            net.send(c_v.at[k, ahead(2), 1], ra.at[k, 1], x=3),
        )

    def y_first_send(k, rel):
        ysent[k, rel] = net.send(c_v.at[k, ahead(rel), other_yh], ry4.at[Y_FIRST.index(k), rel], y=2)

    def x_direct(k):
        direct[k] = (
            net.send(c_v.at[k, ahead(1), 1], rb.at[k, 0, 1], x=1),
            net.send(c_v.at[k, ahead(3), 0], rb.at[k, 1, 0], x=3),
        )

    def x_relay(k):
        sends = []
        for way, rel, by in ((0, 1, 1), (1, 3, 3)):
            far[k][way].wait_recv()
            to = ahead(rel)
            c_v[k, to, way] = (c_v[k, to, way].astype(F32) + ra[k, way].astype(F32)).astype(BF16)
            sends.append(net.send(c_v.at[k, to, way], rb.at[k, way, way], x=by))
        relayed[k] = sends

    def x_total(k, h):
        return c_v[k, x, h].astype(F32) + rb[k, 0, h].astype(F32) + rb[k, 1, h].astype(F32)

    def x_sum(k):
        for copy in (*direct[k], *relayed[k]):
            copy.wait_recv()
        c_v[k, x, other_yh] = x_total(k, other_yh).astype(BF16)
        ysent[k] = net.send(c_v.at[k, x, other_yh], ry.at[k], y=2)

    squares = []
    hg = {}

    def hidden_out(k, hidden):
        cols = pl.ds(k * WIDE, WIDE)
        squares.append(jnp.sum(hidden * hidden, axis=-1, keepdims=True))
        hg_v[k, z, c] = (hidden * gain[:, cols]).astype(BF16)
        ref = hg_v.at[k, z, c]
        hg[k] = {by: net.send(ref, ref, z=by) for by in (1, 3)}
        hg[k]["pair"] = [net.send(ref, ref, c=1)]

    def y_sum(k):
        ysent[k].wait_recv()
        cols = pl.ds(k * WIDE, WIDE)
        hidden_out(k, r_v[:, cols].astype(F32) + x_total(k, yh) + ry[k].astype(F32))

    low, high = pl.ds(0, 80), pl.ds(80, 80)

    def y_first_add(k, rel):
        ysent[k, rel].wait_recv()
        to = ahead(rel)
        c_v[k, to, yh] = (c_v[k, to, yh].astype(F32) + ry4[Y_FIRST.index(k), rel].astype(F32)).astype(BF16)
        return to

    def y_first_far(k):
        to = y_first_add(k, 2)
        far[k] = (
            net.send(c_v.at[k, to, yh, low], ra.at[k, 0, low], x=1),
            net.send(c_v.at[k, to, yh, high], ra.at[k, 1, high], x=3),
        )

    def y_first_direct(k):
        one = net.send(c_v.at[k, y_first_add(k, 1), yh, high], rb.at[k, 0, 0, high], x=1)
        direct[k] = (one, net.send(c_v.at[k, y_first_add(k, 3), yh, low], rb.at[k, 1, 0, low], x=3))

    def y_first_relay(k):
        sends = []
        for way, rel, by, rows in ((0, 1, 1, low), (1, 3, 3, high)):
            far[k][way].wait_recv()
            to = ahead(rel)
            c_v[k, to, yh, rows] = (c_v[k, to, yh, rows].astype(F32) + ra[k, way, rows].astype(F32)).astype(BF16)
            sends.append(net.send(c_v.at[k, to, yh, rows], rb.at[k, way, 0, rows], x=by))
        relayed[k] = sends

    def y_first_out(k):
        for copy in (*direct[k], *relayed[k]):
            copy.wait_recv()
        cols = pl.ds(k * WIDE, WIDE)
        ysent[k, 0].wait_recv()
        total = c_v[k, x, yh].astype(F32) + ry4[Y_FIRST.index(k), 0].astype(F32)
        total = total + rb[k, 0, 0].astype(F32) + rb[k, 1, 0].astype(F32)
        hidden_out(k, r_v[:, cols].astype(F32) + total)

    def hg_on(k):
        hg[k]["on"] = []
        for by, rows in ((1, low), (3, high)):
            source = step(z, 4 - by)
            hg[k][by].wait_recv()
            ref = hg_v.at[k, source, c, rows]
            hg[k]["on"].append(net.send(ref, ref, z=by))
            ref = hg_v.at[k, source, c]
            hg[k]["pair"].append(net.send(ref, ref, c=1))

    def hg_end(k):
        for copy in hg[k]["on"]:
            copy.wait_recv()
        ref = hg_v.at[k, step(z, 2), c]
        hg[k]["pair"].append(net.send(ref, ref, c=1))

    def hg_dot(k):
        for copy in hg[k]["pair"]:
            copy.wait_recv()

        t_v[...] += jnp.dot(
            hg_v[k].reshape(1280, WIDE), p_v[k // 2, k % 2].reshape(WIDE, 256), preferred_element_type=F32
        ).reshape(4, 320, 256)

    def plane_x():
        load_p.wait()
        ref = p_v.at[x, yh, yl]
        return [net.send(ref, ref, x=by) for by in (1, 3, 2)]

    def ws_pair():
        load_ws.wait()
        for copy in ws_z:
            copy.wait_recv()
        copy = net.load(ws_t.at[:, :, mine], ws_v.at[yl, :, c, x, yh])
        return copy, net.send(ws_t.at[:, :, theirs], ws_v.at[yl, :, c, x, yh], c=1)

    def ws_x(pair):
        pair[0].wait()
        pair[1].wait_recv()
        ref = ws_v.at[yl, :, :, x, yh]
        return [net.send(ref, ref, x=by) for by in (1, 3, 2)]

    def p_at(yv, cols):
        return p_v.at[:, lax.div(yv, 2), lax.rem(yv, 2), :, cols]

    def ws_at(yv, cols):
        return ws_v.at[lax.rem(yv, 2), :, :, :, lax.div(yv, 2), :, cols]

    def plane_y(arriving, ref_at):
        for copy in arriving:
            copy.wait_recv()
        ref = ref_at(y, pl.ds(0, 256))
        return {by: net.send(ref, ref, y=by) for by in (1, 3)}

    def plane_y_on(ring, ref_at):
        sends = []
        for by, begin in ((1, 0), (3, 128)):
            ring[by].wait_recv()
            ref = ref_at(step(y, 4 - by), pl.ds(begin, 128))
            sends.append(net.send(ref, ref, y=by))
        return sends

    def s_on():
        sends = []
        for by, rows in ((1, low), (3, high)):
            source = step(z, 4 - by)
            s_ring[by].wait_recv()
            ref = s_v.at[source, c, rows]
            sends.append(net.send(ref, ref, z=by))
            ref = s_v.at[source, c]
            s_pair.append(net.send(ref, ref, c=1))
        return sends

    def s_end(sends):
        for copy in sends:
            copy.wait_recv()
        ref = s_v.at[step(z, 2), c]
        s_pair.append(net.send(ref, ref, c=1))

    def sr_end():
        load_sr.wait()
        for copy in sr_z:
            copy.wait_recv()
        return net.load(sr_t.at[:, :, mine], sr_v.at[:, c]), net.send(sr_t.at[:, :, theirs], sr_v.at[:, c], c=1)

    def student(copies):
        for copy in copies:
            copy.wait_recv()
        so_v[...] = sr_v[...].reshape(4, 320, 256).astype(F32) + jnp.dot(
            s_v[...].reshape(1280, 2048), ws_v[...].reshape(2048, 256), preferred_element_type=F32
        ).reshape(4, 320, 256)

    def transpose():
        load_s.wait()
        for copy in s_pair:
            copy.wait_recv()

        @pl.loop(0, 8)
        def _(j):
            cols = pl.ds(pl.multiple_of(j * 256, 256), 256)
            st_v[cols] = s_v[:, :, :, cols].reshape(1280, 256).T

    load_a.wait()
    t_v[...] = jnp.zeros_like(t_v)
    products(2)
    pl.semaphore_wait(barrier, len(partners))
    p_x = plane_x()
    ws_z = [net.send(ws_in.at[:, slab(step(z, by))], ws_t.at[z], z=by) for by in (1, 3, 2)]
    x_far(2)
    products(3)
    y_first_send(3, 1)
    y_first_send(3, 3)
    sr_z = [net.send(sr_in.at[:, slab(step(z, by))], sr_t.at[z], z=by) for by in (1, 3, 2)]
    y_first_send(3, 2)
    products(6)
    products(7)
    x_direct(2)
    products(1)
    x_relay(2)
    sr_copies = sr_end()
    w_pair = ws_pair()
    y_first_send(3, 0)
    x_far(1)
    p_ring = plane_y(p_x, p_at)
    y_first_direct(3)
    y_first_send(7, 0)
    products(0)
    y_first_far(3)
    y_first_send(7, 2)
    products(4)
    s_ring = {by: net.send(s_in, s_v.at[z, c], z=by) for by in (1, 3)}
    s_pair = [net.send(s_in, s_v.at[z, c], c=1)]
    x_far(0)
    x_far(4)
    y_first_send(7, 1)
    x_far(6)
    x_relay(1)
    x_direct(6)
    x_direct(1)
    x_sum(2)
    load_r.wait()
    y_sum(2)
    products(5)
    x_relay(0)
    x_sum(1)
    s_sends = s_on()
    y_first_relay(3)
    x_direct(0)
    y_sum(1)
    x_relay(6)
    x_direct(4)
    y_first_send(7, 3)
    x_sum(0)
    x_relay(4)
    p_on = plane_y_on(p_ring, p_at)
    hg_on(1)
    y_first_out(3)
    s_end(s_sends)
    x_far(5)
    hg_on(2)
    x_sum(6)
    w_x = ws_x(w_pair)
    y_sum(0)
    x_sum(4)
    y_first_far(7)
    x_direct(5)
    hg_on(3)
    y_sum(6)
    x_relay(5)
    y_sum(4)
    hg_end(3)
    ws_ring = plane_y(w_x, ws_at)
    hg_on(6)
    transpose()
    hg_end(1)
    y_first_direct(7)
    x_sum(5)
    hg_on(0)
    y_first_relay(7)
    hg_end(6)
    hg_end(2)
    hg_on(4)
    y_first_out(7)
    ws_on = plane_y_on(ws_ring, ws_at)
    hg_end(4)
    y_sum(5)
    inverse = lax.rsqrt(sum(squares) * (1.0 / 4096.0) + 1e-05)
    iv_v[z, c] = jnp.broadcast_to(inverse, (160, 128)).T[:8]
    iv_z = [net.send(iv_v.at[z, c], iv_v.at[z, c], z=by) for by in (1, 3, 2)]
    sr_copies[0].wait()
    student(ws_on + [sr_copies[1]])
    hg_end(0)
    hg_on(7)
    for copy in p_on:
        copy.wait_recv()
    hg_dot(6)
    hg_on(5)
    hg_dot(2)
    hg_dot(1)
    hg_dot(4)
    hg_end(7)
    hg_dot(0)
    for copy in iv_z:
        copy.wait_recv()
    iv_pair = net.send(iv_v.at[:, c], iv_v.at[:, c], c=1)
    hg_end(5)
    hg_dot(3)
    hg_dot(7)
    hg_dot(5)
    iv_pair.wait_recv()
    for i in range(4):
        for core in range(2):
            scale = iv_v[i, core].T[:, 0:1]
            rows = pl.ds(core * 160, 160)
            g_v[i, rows] = (128.0 / 20480.0 * (so_v[i, rows] - scale * t_v[i, rows])).astype(BF16)

    @pl.loop(0, 2)
    def _(i):
        rows = pl.ds(pl.multiple_of(i * 1024, 1024), 1024)
        res = jnp.dot(st_v[rows], g_v[...].reshape(1280, 256), preferred_element_type=F32)
        grad[i] = res.astype(BF16).reshape(4, 2, 4, 2, 16, 256)

    left, right = pl.ds(0, 128), pl.ds(128, 128)
    first_x = [net.send(grad.at[:, :, :, step(x, by), :, :, left], ga1.at[by - 1], x=by) for by in (1, 3, 2)]
    first_y = []
    for by in (1, 3, 2):
        to = step(y, by)
        ref = grad.at[lax.rem(to, 2), :, :, :, lax.div(to, 2), :, right]
        first_y.append(net.send(ref, gb1.at[by - 1], y=by))
    for copy in first_x:
        copy.wait_recv()
    total = grad[:, :, :, x, :, :, left].astype(F32)
    ga2[...] = total + ga1[0].astype(F32) + ga1[1].astype(F32) + ga1[2].astype(F32)
    second_y = []
    for by in (1, 3, 2):
        to = step(y, by)
        second_y.append(net.send(ga2.at[lax.rem(to, 2), :, :, lax.div(to, 2)], ra2.at[by - 1], y=by))
    for copy in first_y:
        copy.wait_recv()
    total = grad[yl, :, :, :, yh, :, right].astype(F32)
    gb2[...] = total + gb1[0].astype(F32) + gb1[1].astype(F32) + gb1[2].astype(F32)
    second_x = [net.send(gb2.at[:, :, step(x, by)], rb2.at[by - 1], x=by) for by in (1, 3, 2)]
    for copy in second_y:
        copy.wait_recv()
    fin[:, :, :, left] = ga2[yl, :, :, yh] + ra2[0] + ra2[1] + ra2[2]
    for copy in second_x:
        copy.wait_recv()
    fin[:, :, :, right] = gb2[:, :, x] + rb2[0] + rb2[1] + rb2[2]

    last = []
    for by, core in ((0, 1), (1, 0), (3, 0), (1, 1), (3, 1), (2, 0), (2, 1)):
        ref = fin.at[step(z, by), lax.rem(c + core, 2)]
        last.append(net.send(ref, o_r.at[z, c], z=by, c=core))
    o_r[z, c] = fin[z, c]
    for copy in last:
        copy.wait_recv()
    for i in range(4):
        for core in range(2):
            out[:, pl.ds(i * 512 + core * 256, 256)] = o_r[i, core]

    for copy in net.sent:
        copy.wait_send()


def per_device(a, w, resid, gain, projector, s, s_resid, ws):
    anywhere = pl.BlockSpec(memory_space=pl.ANY)
    vmem = pl.BlockSpec(memory_space=pltpu.VMEM)
    chunks = 4096 // WIDE
    return pl.pallas_call(
        kernel,
        out_shape=jax.ShapeDtypeStruct((16, 2048), F32),
        in_specs=[anywhere, anywhere, anywhere, vmem, anywhere, anywhere, anywhere, anywhere],
        out_specs=vmem,
        scratch_shapes=[
            pltpu.VMEM((4, 320, 1024), BF16),
            pltpu.VMEM((2, 1024, WIDE), BF16),
            pltpu.VMEM((chunks, 4, 2, 160, WIDE), BF16),
            pltpu.VMEM((chunks, 2, 160, WIDE), BF16),
            pltpu.VMEM((chunks, 2, 2, 160, WIDE), BF16),
            pltpu.VMEM((chunks, 160, WIDE), BF16),
            pltpu.VMEM((len(Y_FIRST), 4, 160, WIDE), BF16),
            pltpu.VMEM((160, 4096), BF16),
            pltpu.VMEM((chunks, 4, 2, 160, WIDE), BF16),
            pltpu.VMEM((4, 2, 2, 256, 256), BF16),
            pltpu.VMEM((4, 16, 512), BF16),
            pltpu.VMEM((2, 4, 2, 4, 2, 16, 256), BF16),
            pltpu.VMEM((4, 2, 160, 2048), BF16),
            pltpu.VMEM((2048, 1280), BF16),
            pltpu.VMEM((4, 160, 512), BF16),
            pltpu.VMEM((4, 2, 160, 256), BF16),
            pltpu.VMEM((4, 320, 256), F32),
            pltpu.VMEM((4, 320, 256), F32),
            pltpu.VMEM((4, 320, 256), BF16),
            pltpu.VMEM((4, 2, 8, 160), F32),
            pltpu.VMEM((2, 4, 2, 4, 2, 16, 256), BF16),
            pltpu.VMEM((3, 2, 4, 2, 2, 16, 128), BF16),
            pltpu.VMEM((3, 4, 2, 4, 16, 128), BF16),
            pltpu.VMEM((2, 4, 2, 2, 16, 128), F32),
            pltpu.VMEM((4, 2, 4, 16, 128), F32),
            pltpu.VMEM((3, 4, 2, 16, 128), F32),
            pltpu.VMEM((3, 4, 2, 16, 128), F32),
            pltpu.VMEM((4, 2, 16, 256), F32),
            pltpu.VMEM((4, 2, 16, 256), F32),
            pltpu.SemaphoreType.DMA((N_SEM,)),
            pltpu.SemaphoreType.DMA((N_SEM,)),
            pltpu.SemaphoreType.DMA((N_LOCAL,)),
        ],
        compiler_params=pltpu.CompilerParams(
            collective_id=0, has_side_effects=True, vmem_limit_bytes=62 * 2**20
        ),
        cost_estimate=pl.CostEstimate(flops=16 * 10**9, bytes_accessed=16 * 10**6, transcendentals=160),
    )(
        a.reshape(4, 320, 1024),
        w,
        resid,
        gain.reshape(1, 4096),
        projector.reshape(2, 256, 2048),
        s,
        s_resid,
        ws,
    )


def solution(mesh):
    return jax.shard_map(
        per_device,
        mesh=mesh,
        in_specs=(
            P("dp", "tensor"),
            P("tensor", None),
            P(("dp", "tensor"), None),
            P(),
            P("tensor", None),
            P(("dp", "tensor"), None),
            P(("dp", "tensor"), None),
            P(("dp", "tensor"), None),
        ),
        out_specs=P(("dp", "tensor"), None),
        check_vma=False,
    )
```

```python
import math

import jax
import jax.numpy as jnp
from jax import lax
from jax.experimental import pallas as pl
from jax.experimental.pallas import tpu as pltpu
from jax.sharding import PartitionSpec as P

MESH = pl.DeviceIdType.MESH
BF16 = jnp.bfloat16
F32 = jnp.float32

WIDE = 512
STARTS = (0, 512, 1024, 1536, 2048, 2560, 3072, 3584)
WIDTHS = (512, 512, 512, 512, 512, 512, 512, 512)
Y_FIRST = (3, 7)
W_ORDER = (5, 3, 1, 6, 0, 7, 2, 4)
N_SEND = 14
N_RECV = 76
N_LOCAL = 16


def step(v, by):
    return lax.rem(v + by, 4)


def factors(tiles):
    for rows in range(64, 0, -1):
        if tiles % rows == 0 and tiles // rows <= 32:
            return rows, tiles // rows
    return None


class Net:
    def __init__(self, send_sems, recv_sems, local_sems, ruler):
        dp, t = lax.axis_index("dp"), lax.axis_index("tensor")
        self.x = lax.div(t, 2)
        self.y = lax.rem(t, 2) * 2 + lax.div(dp, 8)
        self.z = lax.rem(lax.div(dp, 2), 4)
        self.c = lax.rem(dp, 2)
        self.send_sems, self.recv_sems, self.local_sems = send_sems, recv_sems, local_sems
        self.ruler = ruler
        self.used_local = 0
        self.keys = {}
        self.sizes = []

    def at(self, x=0, y=0, z=0, c=0):
        px, py, pz = step(self.x, x), step(self.y, y), step(self.z, z)
        pc = lax.rem(self.c + c, 2)
        return (lax.rem(py, 2) * 8 + pz * 2 + pc, px * 2 + lax.div(py, 2))

    def send(self, key, src, dst, **where):
        tiles = math.prod(src.shape) * src.dtype.itemsize // 4096
        index, total = self.keys.get(key, (len(self.keys), 0))
        self.keys[key] = (index, total + tiles)
        for i, (size, count) in enumerate(self.sizes):
            if size == tiles and factors(size * (count + 1)):
                self.sizes[i] = (size, count + 1)
                break
        else:
            i = len(self.sizes)
            self.sizes.append((tiles, 1))
        pltpu.make_async_remote_copy(
            src_ref=src,
            dst_ref=dst,
            send_sem=self.send_sems.at[i],
            recv_sem=self.recv_sems.at[index],
            device_id=self.at(**where),
            device_id_type=MESH,
        ).start()

    def wait_tiles(self, tiles, sem):
        rows, cols = factors(tiles)
        ref = self.ruler.at[pl.ds(0, rows * 16), pl.ds(0, cols * 128)]
        pltpu.make_async_copy(ref, ref, sem).wait()

    def wait(self, key):
        index, tiles = self.keys[key]
        self.wait_tiles(tiles, self.recv_sems.at[index])

    def wait_sent(self):
        for i, (size, count) in enumerate(self.sizes):
            self.wait_tiles(size * count, self.send_sems.at[i])

    def load(self, src, dst):
        i = self.used_local
        self.used_local += 1
        copy = pltpu.make_async_copy(src, dst, self.local_sems.at[i])
        copy.start()
        return copy


def kernel(
    a_in, w_in, r_in, gain, p_in, s_in, sr_in, ws_in, out,
    a_v, w_v, c_v, ra, rb, ry, ry4, r_v, hg_v, p_v, ws_t, ws_v, s_v, st_v, sr_t, sr_v, t_v, so_v, g_v,
    iv_v, grad, ga1, gb1, ga2, gb2, ra2, rb2, fin, o_r,
    send_sems, recv_sems, local_sems,
):
    net = Net(send_sems, recv_sems, local_sems, w_in)
    x, y, z, c = net.x, net.y, net.z, net.c
    other_c = 1 - c
    yh, yl = lax.div(y, 2), lax.rem(y, 2)
    other_yh = 1 - yh
    my_cols = pl.ds(pl.multiple_of(z * 512 + c * 256, 256), 256)
    mine = pl.ds(pl.multiple_of(c * 256, 256), 256)
    theirs = pl.ds(pl.multiple_of(other_c * 256, 256), 256)

    def slab(zv):
        return pl.ds(pl.multiple_of(zv * 512, 512), 512)

    load_a = net.load(a_in, a_v)
    w_loads = {}

    def load_w(n):
        if n < len(W_ORDER):
            k = W_ORDER[n]
            cols = pl.ds(STARTS[k], WIDTHS[k])
            w_loads[n] = net.load(w_in.at[:, cols], w_v.at[n % 2, :, pl.ds(0, WIDTHS[k])])

    load_w(0)

    partners = [dict(c=1)] + [{axis: by} for axis in "xyz" for by in (1, 2, 3)] + [dict(z=by, c=1) for by in (1, 2, 3)]
    barrier = pltpu.get_barrier_semaphore()
    for where in partners:
        pl.semaphore_signal(barrier, inc=1, device_id=net.at(**where), device_id_type=MESH)

    def ahead(by):
        return step(x, by)

    def products(k):
        n = W_ORDER.index(k)
        w_loads[n].wait()

        @pl.loop(0, WIDTHS[k] // 256)
        def _(j):
            cols = pl.ds(pl.multiple_of(j * 256, 256), 256)
            res = jnp.dot(a_v[...].reshape(1280, 1024), w_v[n % 2, :, cols], preferred_element_type=F32)
            c_v[k, :, :, :, cols] = res.astype(BF16).reshape(4, 2, 160, 256)

        load_w(n + 2)

    low, high = pl.ds(0, 80), pl.ds(80, 80)

    def block(ref, *index, rows=pl.ds(0, 160)):
        return ref.at[(*index, rows, pl.ds(0, WIDTHS[index[0]]))]

    def read(ref, *index, rows=pl.ds(0, 160)):
        return block(ref, *index, rows=rows)[...].astype(F32)

    def write(value, ref, *index, rows=pl.ds(0, 160)):
        block(ref, *index, rows=rows)[...] = value.astype(BF16)

    def x_far(k):
        net.send(("far", k), block(c_v, k, ahead(2), 0), block(ra, k, 0), x=1)
        net.send(("far", k), block(c_v, k, ahead(2), 1), block(ra, k, 1), x=3)

    def x_direct(k):
        net.send(("near", k), block(c_v, k, ahead(1), 1), block(rb, k, 0, 1), x=1)
        net.send(("near", k), block(c_v, k, ahead(3), 0), block(rb, k, 1, 0), x=3)

    def x_relay(k):
        net.wait(("far", k))
        for way, rel, by in ((0, 1, 1), (1, 3, 3)):
            to = ahead(rel)
            write(read(c_v, k, to, way) + read(ra, k, way), c_v, k, to, way)
            net.send(("near", k), block(c_v, k, to, way), block(rb, k, way, way), x=by)

    def x_total(k, h):
        return read(c_v, k, x, h) + read(rb, k, 0, h) + read(rb, k, 1, h)

    def x_sum(k):
        net.wait(("near", k))
        write(x_total(k, other_yh), c_v, k, x, other_yh)
        net.send(("y", k), block(c_v, k, x, other_yh), block(ry, k), y=2)

    squares = []

    def hidden_out(k, attended):
        cols = pl.ds(STARTS[k], WIDTHS[k])
        hidden = r_v[:, cols].astype(F32) + attended
        squares.append(jnp.sum(hidden * hidden, axis=-1, keepdims=True))
        write(hidden * gain[:, cols], hg_v, k, z, c)
        ref = block(hg_v, k, z, c)
        for by in (1, 3):
            net.send(("hg", k), ref, ref, z=by)
        net.send(("pair", k), ref, ref, c=1)

    def y_sum(k):
        net.wait(("y", k))
        hidden_out(k, x_total(k, yh) + read(ry, k))

    def y_first_send(k, rel):
        ref = ry4.at[Y_FIRST.index(k), rel, :, pl.ds(0, WIDTHS[k])]
        net.send(("y", k, rel), block(c_v, k, ahead(rel), other_yh), ref, y=2)

    def y_first_add(k, rel):
        net.wait(("y", k, rel))
        ref = ry4.at[Y_FIRST.index(k), rel, :, pl.ds(0, WIDTHS[k])]
        write(read(c_v, k, ahead(rel), yh) + ref[...].astype(F32), c_v, k, ahead(rel), yh)

    def y_first_far(k):
        y_first_add(k, 2)
        net.send(("far", k), block(c_v, k, ahead(2), yh, rows=low), block(ra, k, 0, rows=low), x=1)
        net.send(("far", k), block(c_v, k, ahead(2), yh, rows=high), block(ra, k, 1, rows=high), x=3)

    def y_first_direct(k):
        y_first_add(k, 1)
        net.send(("near", k), block(c_v, k, ahead(1), yh, rows=high), block(rb, k, 0, 0, rows=high), x=1)
        y_first_add(k, 3)
        net.send(("near", k), block(c_v, k, ahead(3), yh, rows=low), block(rb, k, 1, 0, rows=low), x=3)

    def y_first_relay(k):
        net.wait(("far", k))
        for way, rel, by, rows in ((0, 1, 1, low), (1, 3, 3, high)):
            to = ahead(rel)
            write(read(c_v, k, to, yh, rows=rows) + read(ra, k, way, rows=rows), c_v, k, to, yh, rows=rows)
            net.send(("near", k), block(c_v, k, to, yh, rows=rows), block(rb, k, way, 0, rows=rows), x=by)

    def y_first_out(k):
        y_first_add(k, 0)
        net.wait(("near", k))
        hidden_out(k, read(c_v, k, x, yh) + read(rb, k, 0, 0) + read(rb, k, 1, 0))

    def hg_on(k):
        net.wait(("hg", k))
        for by, rows in ((1, low), (3, high)):
            source = step(z, 4 - by)
            ref = block(hg_v, k, source, c, rows=rows)
            net.send(("on", k), ref, ref, z=by)
        for by in (1, 3):
            ref = block(hg_v, k, step(z, 4 - by), c)
            net.send(("pair", k), ref, ref, c=1)

    def hg_end(k):
        net.wait(("on", k))
        ref = block(hg_v, k, step(z, 2), c)
        net.send(("pair", k), ref, ref, c=1)

    def hg_dot(k):
        net.wait(("pair", k))
        start, width = STARTS[k], WIDTHS[k]
        shard = start // 512
        halves = p_v[shard // 2, shard % 2]
        if width == 256:
            halves = halves[start % 512 // 256]
        t_v[...] += jnp.dot(
            hg_v[k, :, :, :, :width].reshape(1280, width),
            halves.reshape(width, 256),
            preferred_element_type=F32,
        ).reshape(4, 320, 256)

    begins = ((1, pl.ds(0, 128)), (3, pl.ds(128, 128)))

    def p_x():
        for by in (1, 3):
            net.send("p_x", p_in.at[yl, :, my_cols], p_v.at[x, yh, yl], x=by)

    def p_x_on():
        net.wait("p_x")
        for by, cols in begins:
            ref = p_v.at[step(x, 4 - by), yh, yl, :, cols]
            net.send("p_x_on", ref, ref, x=by)

    def p_at(yv, cols):
        return p_v.at[:, lax.div(yv, 2), lax.rem(yv, 2), :, cols]

    def p_ring():
        load_p.wait()
        net.wait("p_x_on")
        ref = p_at(y, pl.ds(0, 256))
        for by in (1, 3):
            net.send("p_ring", ref, ref, y=by)

    def p_on():
        net.wait("p_ring")
        for by, cols in begins:
            ref = p_at(step(y, 4 - by), cols)
            net.send("p_on", ref, ref, y=by)

    def ws_z():
        for by in (1, 3, 2):
            net.send("ws_z", ws_in.at[:, slab(step(z, by))], ws_t.at[z], z=by)

    def w_pair():
        load_ws.wait()
        net.wait("ws_z")
        net.send("w_pair", ws_t.at[:, :, theirs], ws_v.at[yl, :, c, x, yh], c=1)
        return net.load(ws_t.at[:, :, mine], ws_v.at[yl, :, c, x, yh])

    def w_x(copy):
        copy.wait()
        net.wait("w_pair")
        ref = ws_v.at[yl, :, :, x, yh]
        for by in (1, 3):
            net.send("w_x", ref, ref, x=by)

    def w_x_on():
        net.wait("w_x")
        for by, cols in begins:
            ref = ws_v.at[yl, :, :, step(x, 4 - by), yh, :, cols]
            net.send("w_x_on", ref, ref, x=by)

    def ws_at(yv, cols):
        return ws_v.at[lax.rem(yv, 2), :, :, :, lax.div(yv, 2), :, cols]

    def ws_ring():
        net.wait("w_x_on")
        ref = ws_at(y, pl.ds(0, 256))
        for by in (1, 3):
            net.send("ws_ring", ref, ref, y=by)

    def ws_on():
        net.wait("ws_ring")
        for by, cols in begins:
            ref = ws_at(step(y, 4 - by), cols)
            net.send("ws_on", ref, ref, y=by)

    def s_ring():
        for by in (1, 3):
            net.send("s_ring", s_in, s_v.at[z, c], z=by)
        net.send("s_pair", s_in, s_v.at[z, c], c=1)

    def s_on():
        net.wait("s_ring")
        for by, rows in ((1, low), (3, high)):
            ref = s_v.at[step(z, 4 - by), c, rows]
            net.send("s_on", ref, ref, z=by)
        for by in (1, 3):
            ref = s_v.at[step(z, 4 - by), c]
            net.send("s_pair", ref, ref, c=1)

    def s_end():
        net.wait("s_on")
        ref = s_v.at[step(z, 2), c]
        net.send("s_pair", ref, ref, c=1)

    def sr_z():
        for by in (1, 3, 2):
            net.send("sr_z", sr_in.at[:, slab(step(z, by))], sr_t.at[z], z=by)

    def sr_end():
        load_sr.wait()
        net.wait("sr_z")
        net.send("sr_pair", sr_t.at[:, :, theirs], sr_v.at[:, c], c=1)
        return net.load(sr_t.at[:, :, mine], sr_v.at[:, c])

    def transpose():
        load_s.wait()
        net.wait("s_pair")

        @pl.loop(0, 8)
        def _(j):
            cols = pl.ds(pl.multiple_of(j * 256, 256), 256)
            st_v[cols] = s_v[:, :, :, cols].reshape(1280, 256).T

    def student(copy):
        copy.wait()
        net.wait("sr_pair")
        net.wait("ws_on")
        so_v[...] = sr_v[...].reshape(4, 320, 256).astype(F32) + jnp.dot(
            s_v[...].reshape(1280, 2048), ws_v[...].reshape(2048, 256), preferred_element_type=F32
        ).reshape(4, 320, 256)

    pl.semaphore_wait(barrier, len(partners))
    p_x()
    ws_z()
    s_ring()
    load_a.wait()
    load_w(1)
    load_p = net.load(p_in.at[yl, :, my_cols], p_v.at[x, yh, yl])
    load_ws = net.load(ws_in.at[:, slab(z)], ws_t.at[z])
    load_sr = net.load(sr_in.at[:, slab(z)], sr_t.at[z])
    load_s = net.load(s_in, s_v.at[z, c])
    load_r = net.load(r_in, r_v)
    t_v[...] = jnp.zeros_like(t_v)
    products(5)
    x_direct(5)
    products(3)
    products(1)
    x_far(5)
    p_x_on()
    x_far(1)
    y_first_send(3, 1)
    y_first_send(3, 2)
    products(6)
    products(0)
    products(7)
    x_far(0)
    y_first_send(3, 0)
    y_first_send(3, 3)
    y_first_send(7, 1)
    x_direct(1)
    y_first_send(7, 2)
    x_relay(1)
    products(2)
    sr_z()
    y_first_far(3)
    x_relay(5)
    y_first_direct(3)
    p_ring()
    x_sum(5)
    x_far(6)
    y_first_send(7, 3)
    s_on()
    w_copy = w_pair()
    y_first_relay(3)
    y_first_far(7)
    x_direct(0)
    x_sum(1)
    load_r.wait()
    y_first_out(3)
    x_relay(0)
    w_x(w_copy)
    x_far(2)
    hg_on(3)
    x_relay(6)
    y_sum(1)
    products(4)
    y_first_direct(7)
    y_first_send(7, 0)
    p_on()
    y_sum(5)
    x_relay(2)
    x_sum(0)
    x_direct(2)
    y_first_relay(7)
    hg_on(1)
    hg_end(1)
    hg_on(5)
    y_first_out(7)
    w_x_on()
    x_direct(6)
    x_sum(2)
    hg_end(5)
    y_sum(0)
    x_far(4)
    x_sum(6)
    hg_on(7)
    x_direct(4)
    hg_end(3)
    net.wait("p_on")
    hg_dot(1)
    y_sum(2)
    s_end()
    ws_ring()
    x_relay(4)
    hg_on(0)
    y_sum(6)
    x_sum(4)
    sr_copy = sr_end()
    hg_end(0)
    hg_dot(5)
    transpose()
    hg_end(7)
    hg_on(2)
    hg_on(6)
    hg_dot(3)
    y_sum(4)
    hg_end(2)
    ws_on()
    hg_dot(2)
    hg_end(6)
    hg_dot(7)
    hg_dot(0)
    inverse = lax.rsqrt(sum(squares) * (1.0 / 4096.0) + 1e-05)
    iv_v[z, c, :, 0:160] = jnp.broadcast_to(inverse, (160, 128)).T[:8]
    for by in (1, 3, 2):
        net.send("scale", iv_v.at[z, c], iv_v.at[z, c], z=by)
    hg_on(4)
    student(sr_copy)
    hg_end(4)
    hg_dot(6)
    net.wait("scale")
    net.send("scale_pair", iv_v.at[:, c], iv_v.at[:, c], c=1)
    hg_dot(4)
    net.wait("scale_pair")
    for i in range(4):
        for core in range(2):
            scale = iv_v[i, core, :, 0:160].T[:, 0:1]
            rows = pl.ds(core * 160, 160)
            g_v[i, rows] = (128.0 / 20480.0 * (so_v[i, rows] - scale * t_v[i, rows])).astype(BF16)

    left, right = pl.ds(0, 128), pl.ds(128, 128)
    for half, near in ((1 - yl, (1, 3)), (yl, (2,))):
        rows = pl.ds(pl.multiple_of(half * 1024, 1024), 1024)
        res = jnp.dot(st_v[rows], g_v[...].reshape(1280, 256), preferred_element_type=F32)
        grad[half] = res.astype(BF16).reshape(4, 2, 4, 2, 16, 256)
        for by in near:
            ref = grad.at[half, :, :, :, lax.div(step(y, by), 2), :, right]
            net.send("y_1", ref, gb1.at[by - 1], y=by)
        for by in (1, 3, 2):
            net.send("x_1", grad.at[half, :, :, step(x, by), :, :, left], ga1.at[by - 1, half], x=by)

    def four(own, others):
        return own.astype(F32) + others[0].astype(F32) + others[1].astype(F32) + others[2].astype(F32)

    net.wait("x_1")
    ga2[...] = four(grad[:, :, :, x, :, :, left], ga1).astype(BF16)
    for by in (1, 3, 2):
        to = step(y, by)
        net.send("y_2", ga2.at[lax.rem(to, 2), :, :, lax.div(to, 2)], ra2.at[by - 1], y=by)
    net.wait("y_1")
    gb2[...] = four(grad[yl, :, :, :, yh, :, right], gb1).astype(BF16)
    for by in (1, 3, 2):
        net.send("x_2", gb2.at[:, :, step(x, by)], rb2.at[by - 1], x=by)
    net.wait("y_2")
    fin[:, :, :, left] = four(ga2[yl, :, :, yh], ra2)
    net.wait("x_2")
    fin[:, :, :, right] = four(gb2[:, :, x], rb2)

    for by, core in ((0, 1), (1, 0), (3, 0), (1, 1), (3, 1), (2, 0), (2, 1)):
        ref = fin.at[step(z, by), lax.rem(c + core, 2)]
        net.send("rows", ref, o_r.at[z, c], z=by, c=core)
    o_r[z, c] = fin[z, c]
    net.wait("rows")
    for i in range(4):
        for core in range(2):
            out[:, pl.ds(i * 512 + core * 256, 256)] = o_r[i, core]

    net.wait_sent()


def per_device(a, w, resid, gain, projector, s, s_resid, ws):
    anywhere = pl.BlockSpec(memory_space=pl.ANY)
    vmem = pl.BlockSpec(memory_space=pltpu.VMEM)
    chunks = len(WIDTHS)
    return pl.pallas_call(
        kernel,
        out_shape=jax.ShapeDtypeStruct((16, 2048), F32),
        in_specs=[anywhere, anywhere, anywhere, vmem, anywhere, anywhere, anywhere, anywhere],
        out_specs=vmem,
        scratch_shapes=[
            pltpu.VMEM((4, 320, 1024), BF16),
            pltpu.VMEM((2, 1024, WIDE), BF16),
            pltpu.VMEM((chunks, 4, 2, 160, WIDE), BF16),
            pltpu.VMEM((chunks, 2, 160, WIDE), BF16),
            pltpu.VMEM((chunks, 2, 2, 160, WIDE), BF16),
            pltpu.VMEM((chunks, 160, WIDE), BF16),
            pltpu.VMEM((len(Y_FIRST), 4, 160, WIDE), BF16),
            pltpu.VMEM((160, 4096), BF16),
            pltpu.VMEM((chunks, 4, 2, 160, WIDE), BF16),
            pltpu.VMEM((4, 2, 2, 256, 256), BF16),
            pltpu.VMEM((4, 16, 512), BF16),
            pltpu.VMEM((2, 4, 2, 4, 2, 16, 256), BF16),
            pltpu.VMEM((4, 2, 160, 2048), BF16),
            pltpu.VMEM((2048, 1280), BF16),
            pltpu.VMEM((4, 160, 512), BF16),
            pltpu.VMEM((4, 2, 160, 256), BF16),
            pltpu.VMEM((4, 320, 256), F32),
            pltpu.VMEM((4, 320, 256), F32),
            pltpu.VMEM((4, 320, 256), BF16),
            pltpu.VMEM((4, 2, 8, 256), F32),
            pltpu.VMEM((2, 4, 2, 4, 2, 16, 256), BF16),
            pltpu.VMEM((3, 2, 4, 2, 2, 16, 128), BF16),
            pltpu.VMEM((3, 4, 2, 4, 16, 128), BF16),
            pltpu.VMEM((2, 4, 2, 2, 16, 128), BF16),
            pltpu.VMEM((4, 2, 4, 16, 128), BF16),
            pltpu.VMEM((3, 4, 2, 16, 128), BF16),
            pltpu.VMEM((3, 4, 2, 16, 128), BF16),
            pltpu.VMEM((4, 2, 16, 256), F32),
            pltpu.VMEM((4, 2, 16, 256), F32),
            pltpu.SemaphoreType.DMA((N_SEND,)),
            pltpu.SemaphoreType.DMA((N_RECV,)),
            pltpu.SemaphoreType.DMA((N_LOCAL,)),
        ],
        compiler_params=pltpu.CompilerParams(
            collective_id=0, has_side_effects=True, vmem_limit_bytes=62 * 2**20
        ),
        cost_estimate=pl.CostEstimate(flops=16 * 10**9, bytes_accessed=16 * 10**6, transcendentals=160),
    )(
        a.reshape(4, 320, 1024),
        w,
        resid,
        gain.reshape(1, 4096),
        projector.reshape(2, 256, 2048),
        s,
        s_resid,
        ws,
    )


def solution(mesh):
    return jax.shard_map(
        per_device,
        mesh=mesh,
        in_specs=(
            P("dp", "tensor"),
            P("tensor", None),
            P(("dp", "tensor"), None),
            P(),
            P("tensor", None),
            P(("dp", "tensor"), None),
            P(("dp", "tensor"), None),
            P(("dp", "tensor"), None),
        ),
        out_specs=P(("dp", "tensor"), None),
        check_vma=False,
    )
```

```python
import math

import jax
import jax.numpy as jnp
from jax import lax
from jax.experimental import pallas as pl
from jax.experimental.pallas import tpu as pltpu
from jax.sharding import PartitionSpec as P

MESH = pl.DeviceIdType.MESH
BF16 = jnp.bfloat16
F32 = jnp.float32

WIDE = 512
STARTS = (0, 512, 1024, 1536, 2048, 2560, 3072, 3584)
WIDTHS = (512, 512, 512, 512, 512, 512, 512, 512)
Y_FIRST = (3, 7)
W_ORDER = (5, 3, 1, 6, 0, 7, 2, 4)
N_SEND = 14
N_RECV = 76
N_LOCAL = 16


def step(v, by):
    return lax.rem(v + by, 4)


def factors(tiles):
    for rows in range(64, 0, -1):
        if tiles % rows == 0 and tiles // rows <= 32:
            return rows, tiles // rows
    return None


class Net:
    def __init__(self, send_sems, recv_sems, local_sems, ruler):
        dp, t = lax.axis_index("dp"), lax.axis_index("tensor")
        self.x = lax.div(t, 2)
        self.y = lax.rem(t, 2) * 2 + lax.div(dp, 8)
        self.z = lax.rem(lax.div(dp, 2), 4)
        self.c = lax.rem(dp, 2)
        self.send_sems, self.recv_sems, self.local_sems = send_sems, recv_sems, local_sems
        self.ruler = ruler
        self.used_local = 0
        self.keys = {}
        self.sizes = []

    def at(self, x=0, y=0, z=0, c=0):
        px, py, pz = step(self.x, x), step(self.y, y), step(self.z, z)
        pc = lax.rem(self.c + c, 2)
        return (lax.rem(py, 2) * 8 + pz * 2 + pc, px * 2 + lax.div(py, 2))

    def send(self, key, src, dst, **where):
        tiles = math.prod(src.shape) * src.dtype.itemsize // 4096
        index, total = self.keys.get(key, (len(self.keys), 0))
        self.keys[key] = (index, total + tiles)
        for i, (size, count) in enumerate(self.sizes):
            if size == tiles and factors(size * (count + 1)):
                self.sizes[i] = (size, count + 1)
                break
        else:
            i = len(self.sizes)
            self.sizes.append((tiles, 1))
        pltpu.make_async_remote_copy(
            src_ref=src,
            dst_ref=dst,
            send_sem=self.send_sems.at[i],
            recv_sem=self.recv_sems.at[index],
            device_id=self.at(**where),
            device_id_type=MESH,
        ).start()

    def wait_tiles(self, tiles, sem):
        rows, cols = factors(tiles)
        ref = self.ruler.at[pl.ds(0, rows * 16), pl.ds(0, cols * 128)]
        pltpu.make_async_copy(ref, ref, sem).wait()

    def wait(self, key):
        index, tiles = self.keys[key]
        self.wait_tiles(tiles, self.recv_sems.at[index])

    def wait_sent(self):
        for i, (size, count) in enumerate(self.sizes):
            self.wait_tiles(size * count, self.send_sems.at[i])

    def load(self, src, dst):
        i = self.used_local
        self.used_local += 1
        copy = pltpu.make_async_copy(src, dst, self.local_sems.at[i])
        copy.start()
        return copy


def kernel(
    a_in, w_in, r_in, gain, p_in, s_in, sr_in, ws_in, out,
    a_v, w_v, c_v, ra, rb, ry, ry4, r_v, hg_v, p_v, ws_t, ws_v, s_v, st_v, sr_t, sr_v, t_v, so_v, g_v,
    iv_v, grad, ga1, gb1, ga2, gb2, ra2, rb2, fin, o_r,
    send_sems, recv_sems, local_sems,
):
    net = Net(send_sems, recv_sems, local_sems, w_in)
    x, y, z, c = net.x, net.y, net.z, net.c
    other_c = 1 - c
    yh, yl = lax.div(y, 2), lax.rem(y, 2)
    other_yh = 1 - yh
    my_cols = pl.ds(pl.multiple_of(z * 512 + c * 256, 256), 256)
    mine = pl.ds(pl.multiple_of(c * 256, 256), 256)
    theirs = pl.ds(pl.multiple_of(other_c * 256, 256), 256)

    def slab(zv):
        return pl.ds(pl.multiple_of(zv * 512, 512), 512)

    load_a = net.load(a_in, a_v)
    w_loads = {}

    def load_w(n):
        if n < len(W_ORDER):
            k = W_ORDER[n]
            cols = pl.ds(STARTS[k], WIDTHS[k])
            w_loads[n] = net.load(w_in.at[:, cols], w_v.at[n % 2, :, pl.ds(0, WIDTHS[k])])

    load_w(0)

    partners = [dict(c=1)] + [{axis: by} for axis in "xyz" for by in (1, 2, 3)] + [dict(z=by, c=1) for by in (1, 2, 3)]
    barrier = pltpu.get_barrier_semaphore()
    for where in partners:
        pl.semaphore_signal(barrier, inc=1, device_id=net.at(**where), device_id_type=MESH)

    def ahead(by):
        return step(x, by)

    def products(k):
        n = W_ORDER.index(k)
        w_loads[n].wait()

        @pl.loop(0, WIDTHS[k] // 256)
        def _(j):
            cols = pl.ds(pl.multiple_of(j * 256, 256), 256)
            res = jnp.dot(a_v[...].reshape(1280, 1024), w_v[n % 2, :, cols], preferred_element_type=F32)
            c_v[k, :, :, :, cols] = res.astype(BF16).reshape(4, 2, 160, 256)

        load_w(n + 2)

    low, high = pl.ds(0, 80), pl.ds(80, 80)

    def block(ref, *index, rows=pl.ds(0, 160)):
        return ref.at[(*index, rows, pl.ds(0, WIDTHS[index[0]]))]

    def read(ref, *index, rows=pl.ds(0, 160)):
        return block(ref, *index, rows=rows)[...].astype(F32)

    def write(value, ref, *index, rows=pl.ds(0, 160)):
        block(ref, *index, rows=rows)[...] = value.astype(BF16)

    def x_far(k):
        net.send(("far", k), block(c_v, k, ahead(2), 0), block(ra, k, 0), x=1)
        net.send(("far", k), block(c_v, k, ahead(2), 1), block(ra, k, 1), x=3)

    def x_direct(k):
        net.send(("near", k), block(c_v, k, ahead(1), 1), block(rb, k, 0, 1), x=1)
        net.send(("near", k), block(c_v, k, ahead(3), 0), block(rb, k, 1, 0), x=3)

    def x_relay(k):
        net.wait(("far", k))
        for way, rel, by in ((0, 1, 1), (1, 3, 3)):
            to = ahead(rel)
            write(read(c_v, k, to, way) + read(ra, k, way), c_v, k, to, way)
            net.send(("near", k), block(c_v, k, to, way), block(rb, k, way, way), x=by)

    def x_total(k, h):
        return read(c_v, k, x, h) + read(rb, k, 0, h) + read(rb, k, 1, h)

    def x_sum(k):
        net.wait(("near", k))
        write(x_total(k, other_yh), c_v, k, x, other_yh)
        net.send(("y", k), block(c_v, k, x, other_yh), block(ry, k), y=2)

    squares = []

    def hidden_out(k, attended):
        cols = pl.ds(STARTS[k], WIDTHS[k])
        hidden = r_v[:, cols].astype(F32) + attended
        squares.append(jnp.sum(hidden * hidden, axis=-1, keepdims=True))
        write(hidden * gain[:, cols], hg_v, k, z, c)
        ref = block(hg_v, k, z, c)
        for by in (1, 3):
            net.send(("hg", k), ref, ref, z=by)
        net.send(("pair", k), ref, ref, c=1)

    def y_sum(k):
        net.wait(("y", k))
        hidden_out(k, x_total(k, yh) + read(ry, k))

    def y_first_send(k, rel):
        ref = ry4.at[Y_FIRST.index(k), rel, :, pl.ds(0, WIDTHS[k])]
        net.send(("y", k, rel), block(c_v, k, ahead(rel), other_yh), ref, y=2)

    def y_first_add(k, rel):
        net.wait(("y", k, rel))
        ref = ry4.at[Y_FIRST.index(k), rel, :, pl.ds(0, WIDTHS[k])]
        write(read(c_v, k, ahead(rel), yh) + ref[...].astype(F32), c_v, k, ahead(rel), yh)

    def y_first_far(k):
        y_first_add(k, 2)
        net.send(("far", k), block(c_v, k, ahead(2), yh, rows=low), block(ra, k, 0, rows=low), x=1)
        net.send(("far", k), block(c_v, k, ahead(2), yh, rows=high), block(ra, k, 1, rows=high), x=3)

    def y_first_direct(k):
        y_first_add(k, 1)
        net.send(("near", k), block(c_v, k, ahead(1), yh, rows=high), block(rb, k, 0, 0, rows=high), x=1)
        y_first_add(k, 3)
        net.send(("near", k), block(c_v, k, ahead(3), yh, rows=low), block(rb, k, 1, 0, rows=low), x=3)

    def y_first_relay(k):
        net.wait(("far", k))
        for way, rel, by, rows in ((0, 1, 1, low), (1, 3, 3, high)):
            to = ahead(rel)
            write(read(c_v, k, to, yh, rows=rows) + read(ra, k, way, rows=rows), c_v, k, to, yh, rows=rows)
            net.send(("near", k), block(c_v, k, to, yh, rows=rows), block(rb, k, way, 0, rows=rows), x=by)

    def y_first_out(k):
        y_first_add(k, 0)
        net.wait(("near", k))
        hidden_out(k, read(c_v, k, x, yh) + read(rb, k, 0, 0) + read(rb, k, 1, 0))

    def hg_on(k):
        net.wait(("hg", k))
        for by, rows in ((1, low), (3, high)):
            source = step(z, 4 - by)
            ref = block(hg_v, k, source, c, rows=rows)
            net.send(("on", k), ref, ref, z=by)
        for by in (1, 3):
            ref = block(hg_v, k, step(z, 4 - by), c)
            net.send(("pair", k), ref, ref, c=1)

    def hg_end(k):
        net.wait(("on", k))
        ref = block(hg_v, k, step(z, 2), c)
        net.send(("pair", k), ref, ref, c=1)

    def hg_dot(k):
        net.wait(("pair", k))
        start, width = STARTS[k], WIDTHS[k]
        shard = start // 512
        halves = p_v[shard // 2, shard % 2]
        if width == 256:
            halves = halves[start % 512 // 256]
        t_v[...] += jnp.dot(
            hg_v[k, :, :, :, :width].reshape(1280, width),
            halves.reshape(width, 256),
            preferred_element_type=F32,
        ).reshape(4, 320, 256)

    begins = ((1, pl.ds(0, 128)), (3, pl.ds(128, 128)))

    def p_x():
        for by in (1, 3):
            net.send("p_x", p_in.at[yl, :, my_cols], p_v.at[x, yh, yl], x=by)

    def p_x_on():
        net.wait("p_x")
        for by, cols in begins:
            ref = p_v.at[step(x, 4 - by), yh, yl, :, cols]
            net.send("p_x_on", ref, ref, x=by)

    def p_at(yv, cols):
        return p_v.at[:, lax.div(yv, 2), lax.rem(yv, 2), :, cols]

    def p_ring():
        load_p.wait()
        net.wait("p_x_on")
        ref = p_at(y, pl.ds(0, 256))
        for by in (1, 3):
            net.send("p_ring", ref, ref, y=by)

    def p_on():
        net.wait("p_ring")
        for by, cols in begins:
            ref = p_at(step(y, 4 - by), cols)
            net.send("p_on", ref, ref, y=by)

    def ws_z():
        for by in (1, 3, 2):
            net.send("ws_z", ws_in.at[:, slab(step(z, by))], ws_t.at[z], z=by)

    def w_pair():
        load_ws.wait()
        net.wait("ws_z")
        net.send("w_pair", ws_t.at[:, :, theirs], ws_v.at[yl, :, c, x, yh], c=1)
        return net.load(ws_t.at[:, :, mine], ws_v.at[yl, :, c, x, yh])

    def w_x(copy):
        copy.wait()
        net.wait("w_pair")
        ref = ws_v.at[yl, :, :, x, yh]
        for by in (1, 3):
            net.send("w_x", ref, ref, x=by)

    def w_x_on():
        net.wait("w_x")
        for by, cols in begins:
            ref = ws_v.at[yl, :, :, step(x, 4 - by), yh, :, cols]
            net.send("w_x_on", ref, ref, x=by)

    def ws_at(yv, cols):
        return ws_v.at[lax.rem(yv, 2), :, :, :, lax.div(yv, 2), :, cols]

    def ws_ring():
        net.wait("w_x_on")
        ref = ws_at(y, pl.ds(0, 256))
        for by in (1, 3):
            net.send("ws_ring", ref, ref, y=by)

    def ws_on():
        net.wait("ws_ring")
        for by, cols in begins:
            ref = ws_at(step(y, 4 - by), cols)
            net.send("ws_on", ref, ref, y=by)

    def s_ring():
        for by in (1, 3):
            net.send("s_ring", s_in, s_v.at[z, c], z=by)
        net.send("s_pair", s_in, s_v.at[z, c], c=1)

    def s_on():
        net.wait("s_ring")
        for by, rows in ((1, low), (3, high)):
            ref = s_v.at[step(z, 4 - by), c, rows]
            net.send("s_on", ref, ref, z=by)
        for by in (1, 3):
            ref = s_v.at[step(z, 4 - by), c]
            net.send("s_pair", ref, ref, c=1)

    def s_end():
        net.wait("s_on")
        ref = s_v.at[step(z, 2), c]
        net.send("s_pair", ref, ref, c=1)

    def sr_z():
        for by in (1, 3, 2):
            net.send("sr_z", sr_in.at[:, slab(step(z, by))], sr_t.at[z], z=by)

    def sr_end():
        load_sr.wait()
        net.wait("sr_z")
        net.send("sr_pair", sr_t.at[:, :, theirs], sr_v.at[:, c], c=1)
        return net.load(sr_t.at[:, :, mine], sr_v.at[:, c])

    def transpose():
        load_s.wait()
        net.wait("s_pair")

        @pl.loop(0, 8)
        def _(j):
            cols = pl.ds(pl.multiple_of(j * 256, 256), 256)
            st_v[cols] = s_v[:, :, :, cols].reshape(1280, 256).T

    def student(copy):
        copy.wait()
        net.wait("sr_pair")
        net.wait("ws_on")

        @pl.loop(0, 4)
        def _(i):
            so_v[i] = sr_v[i].reshape(320, 256).astype(F32) + jnp.dot(
                s_v[i].reshape(320, 2048), ws_v[...].reshape(2048, 256), preferred_element_type=F32
            )


    pl.semaphore_wait(barrier, len(partners))
    p_x()
    ws_z()
    s_ring()
    load_a.wait()
    load_w(1)
    load_p = net.load(p_in.at[yl, :, my_cols], p_v.at[x, yh, yl])
    load_ws = net.load(ws_in.at[:, slab(z)], ws_t.at[z])
    load_sr = net.load(sr_in.at[:, slab(z)], sr_t.at[z])
    load_s = net.load(s_in, s_v.at[z, c])
    load_r = net.load(r_in, r_v)
    t_v[...] = jnp.zeros_like(t_v)
    products(5)
    x_direct(5)
    products(3)
    products(1)
    x_far(5)
    p_x_on()
    x_far(1)
    y_first_send(3, 1)
    y_first_send(3, 2)
    products(6)
    products(0)
    products(7)
    x_far(0)
    y_first_send(3, 0)
    y_first_send(3, 3)
    y_first_send(7, 1)
    x_direct(1)
    y_first_send(7, 2)
    x_relay(1)
    products(2)
    sr_z()
    y_first_far(3)
    x_relay(5)
    y_first_direct(3)
    p_ring()
    x_sum(5)
    x_far(6)
    y_first_send(7, 3)
    s_on()
    w_copy = w_pair()
    y_first_relay(3)
    y_first_far(7)
    x_direct(0)
    x_sum(1)
    load_r.wait()
    y_first_out(3)
    x_relay(0)
    w_x(w_copy)
    x_far(2)
    hg_on(3)
    x_relay(6)
    y_sum(1)
    products(4)
    y_first_direct(7)
    y_first_send(7, 0)
    p_on()
    y_sum(5)
    x_relay(2)
    x_sum(0)
    x_direct(2)
    y_first_relay(7)
    hg_on(1)
    hg_end(1)
    hg_on(5)
    y_first_out(7)
    w_x_on()
    x_direct(6)
    x_sum(2)
    hg_end(5)
    y_sum(0)
    x_far(4)
    x_sum(6)
    hg_on(7)
    x_direct(4)
    hg_end(3)
    net.wait("p_on")
    hg_dot(1)
    y_sum(2)
    s_end()
    ws_ring()
    x_relay(4)
    hg_on(0)
    y_sum(6)
    x_sum(4)
    sr_copy = sr_end()
    hg_end(0)
    hg_dot(5)
    transpose()
    hg_end(7)
    hg_on(2)
    hg_on(6)
    hg_dot(3)
    y_sum(4)
    hg_end(2)
    ws_on()
    hg_dot(2)
    hg_end(6)
    hg_dot(7)
    hg_dot(0)
    inverse = lax.rsqrt(sum(squares) * (1.0 / 4096.0) + 1e-05)
    iv_v[z, c, :, 0:160] = jnp.broadcast_to(inverse, (160, 128)).T[:8]
    for by in (1, 3, 2):
        net.send("scale", iv_v.at[z, c], iv_v.at[z, c], z=by)
    hg_on(4)
    student(sr_copy)
    hg_end(4)
    hg_dot(6)
    net.wait("scale")
    net.send("scale_pair", iv_v.at[:, c], iv_v.at[:, c], c=1)
    hg_dot(4)
    net.wait("scale_pair")
    for i in range(4):
        for core in range(2):
            scale = iv_v[i, core, :, 0:160].T[:, 0:1]
            rows = pl.ds(core * 160, 160)
            g_v[i, rows] = (128.0 / 20480.0 * (so_v[i, rows] - scale * t_v[i, rows])).astype(BF16)

    left, right = pl.ds(0, 128), pl.ds(128, 128)
    for half, near in ((1 - yl, (1, 3)), (yl, (2,))):

        @pl.loop(0, 2)
        def _(i):
            rows = pl.ds(pl.multiple_of(half * 1024 + i * 512, 512), 512)
            res = jnp.dot(st_v[rows], g_v[...].reshape(1280, 256), preferred_element_type=F32)
            grad[half, pl.ds(i * 2, 2)] = res.astype(BF16).reshape(2, 2, 4, 2, 16, 256)

        for by in near:
            ref = grad.at[half, :, :, :, lax.div(step(y, by), 2), :, right]
            net.send("y_1", ref, gb1.at[by - 1], y=by)
        for by in (1, 3, 2):
            net.send("x_1", grad.at[half, :, :, step(x, by), :, :, left], ga1.at[by - 1, half], x=by)

    def four(own, others):
        return own.astype(F32) + others[0].astype(F32) + others[1].astype(F32) + others[2].astype(F32)

    net.wait("x_1")
    ga2[...] = four(grad[:, :, :, x, :, :, left], ga1).astype(BF16)
    for by in (1, 3, 2):
        to = step(y, by)
        net.send("y_2", ga2.at[lax.rem(to, 2), :, :, lax.div(to, 2)], ra2.at[by - 1], y=by)
    net.wait("y_1")
    gb2[...] = four(grad[yl, :, :, :, yh, :, right], gb1).astype(BF16)
    for by in (1, 3, 2):
        net.send("x_2", gb2.at[:, :, step(x, by)], rb2.at[by - 1], x=by)
    net.wait("y_2")
    fin[:, :, :, left] = four(ga2[yl, :, :, yh], ra2)
    net.wait("x_2")
    fin[:, :, :, right] = four(gb2[:, :, x], rb2)

    for by, core in ((0, 1), (1, 0), (3, 0), (1, 1), (3, 1), (2, 0), (2, 1)):
        ref = fin.at[step(z, by), lax.rem(c + core, 2)]
        net.send("rows", ref, o_r.at[z, c], z=by, c=core)
    o_r[z, c] = fin[z, c]
    net.wait("rows")
    for i in range(4):
        for core in range(2):
            out[:, pl.ds(i * 512 + core * 256, 256)] = o_r[i, core]

    net.wait_sent()


def per_device(a, w, resid, gain, projector, s, s_resid, ws):
    anywhere = pl.BlockSpec(memory_space=pl.ANY)
    vmem = pl.BlockSpec(memory_space=pltpu.VMEM)
    chunks = len(WIDTHS)
    return pl.pallas_call(
        kernel,
        out_shape=jax.ShapeDtypeStruct((16, 2048), F32),
        in_specs=[anywhere, anywhere, anywhere, vmem, anywhere, anywhere, anywhere, anywhere],
        out_specs=vmem,
        scratch_shapes=[
            pltpu.VMEM((4, 320, 1024), BF16),
            pltpu.VMEM((2, 1024, WIDE), BF16),
            pltpu.VMEM((chunks, 4, 2, 160, WIDE), BF16),
            pltpu.VMEM((chunks, 2, 160, WIDE), BF16),
            pltpu.VMEM((chunks, 2, 2, 160, WIDE), BF16),
            pltpu.VMEM((chunks, 160, WIDE), BF16),
            pltpu.VMEM((len(Y_FIRST), 4, 160, WIDE), BF16),
            pltpu.VMEM((160, 4096), BF16),
            pltpu.VMEM((chunks, 4, 2, 160, WIDE), BF16),
            pltpu.VMEM((4, 2, 2, 256, 256), BF16),
            pltpu.VMEM((4, 16, 512), BF16),
            pltpu.VMEM((2, 4, 2, 4, 2, 16, 256), BF16),
            pltpu.VMEM((4, 2, 160, 2048), BF16),
            pltpu.VMEM((2048, 1280), BF16),
            pltpu.VMEM((4, 160, 512), BF16),
            pltpu.VMEM((4, 2, 160, 256), BF16),
            pltpu.VMEM((4, 320, 256), F32),
            pltpu.VMEM((4, 320, 256), F32),
            pltpu.VMEM((4, 320, 256), BF16),
            pltpu.VMEM((4, 2, 8, 256), F32),
            pltpu.VMEM((2, 4, 2, 4, 2, 16, 256), BF16),
            pltpu.VMEM((3, 2, 4, 2, 2, 16, 128), BF16),
            pltpu.VMEM((3, 4, 2, 4, 16, 128), BF16),
            pltpu.VMEM((2, 4, 2, 2, 16, 128), BF16),
            pltpu.VMEM((4, 2, 4, 16, 128), BF16),
            pltpu.VMEM((3, 4, 2, 16, 128), BF16),
            pltpu.VMEM((3, 4, 2, 16, 128), BF16),
            pltpu.VMEM((4, 2, 16, 256), F32),
            pltpu.VMEM((4, 2, 16, 256), F32),
            pltpu.SemaphoreType.DMA((N_SEND,)),
            pltpu.SemaphoreType.DMA((N_RECV,)),
            pltpu.SemaphoreType.DMA((N_LOCAL,)),
        ],
        compiler_params=pltpu.CompilerParams(
            collective_id=0, has_side_effects=True, vmem_limit_bytes=62 * 2**20
        ),
        cost_estimate=pl.CostEstimate(flops=16 * 10**9, bytes_accessed=16 * 10**6, transcendentals=160),
    )(
        a.reshape(4, 320, 1024),
        w,
        resid,
        gain.reshape(1, 4096),
        projector.reshape(2, 256, 2048),
        s,
        s_resid,
        ws,
    )


def solution(mesh):
    return jax.shard_map(
        per_device,
        mesh=mesh,
        in_specs=(
            P("dp", "tensor"),
            P("tensor", None),
            P(("dp", "tensor"), None),
            P(),
            P("tensor", None),
            P(("dp", "tensor"), None),
            P(("dp", "tensor"), None),
            P(("dp", "tensor"), None),
        ),
        out_specs=P(("dp", "tensor"), None),
        check_vma=False,
    )
```

```python
import math

import jax
import jax.numpy as jnp
from jax import lax
from jax.experimental import pallas as pl
from jax.experimental.pallas import tpu as pltpu
from jax.sharding import PartitionSpec as P

MESH = pl.DeviceIdType.MESH
BF16 = jnp.bfloat16
F32 = jnp.float32

WIDE = 512
STARTS = (0, 512, 1024, 1536, 2048, 2560, 3072, 3584)
WIDTHS = (512, 512, 512, 512, 512, 512, 512, 512)
Y_FIRST = (3, 7)
W_ORDER = (5, 3, 1, 6, 0, 7, 2, 4)
N_SEND = 14
N_RECV = 76
N_LOCAL = 16


def step(v, by):
    return lax.rem(v + by, 4)


def factors(tiles):
    for rows in range(64, 0, -1):
        if tiles % rows == 0 and tiles // rows <= 32:
            return rows, tiles // rows
    return None


class Net:
    def __init__(self, send_sems, recv_sems, local_sems, ruler):
        dp, t = lax.axis_index("dp"), lax.axis_index("tensor")
        self.x = lax.div(t, 2)
        self.y = lax.rem(t, 2) * 2 + lax.div(dp, 8)
        self.z = lax.rem(lax.div(dp, 2), 4)
        self.c = lax.rem(dp, 2)
        self.send_sems, self.recv_sems, self.local_sems = send_sems, recv_sems, local_sems
        self.ruler = ruler
        self.used_local = 0
        self.keys = {}
        self.sizes = []

    def at(self, x=0, y=0, z=0, c=0):
        px, py, pz = step(self.x, x), step(self.y, y), step(self.z, z)
        pc = lax.rem(self.c + c, 2)
        return (lax.rem(py, 2) * 8 + pz * 2 + pc, px * 2 + lax.div(py, 2))

    def send(self, key, src, dst, **where):
        tiles = math.prod(src.shape) * src.dtype.itemsize // 4096
        index, total = self.keys.get(key, (len(self.keys), 0))
        self.keys[key] = (index, total + tiles)
        for i, (size, count) in enumerate(self.sizes):
            if size == tiles and factors(size * (count + 1)):
                self.sizes[i] = (size, count + 1)
                break
        else:
            i = len(self.sizes)
            self.sizes.append((tiles, 1))
        pltpu.make_async_remote_copy(
            src_ref=src,
            dst_ref=dst,
            send_sem=self.send_sems.at[i],
            recv_sem=self.recv_sems.at[index],
            device_id=self.at(**where),
            device_id_type=MESH,
        ).start()

    def wait_tiles(self, tiles, sem):
        rows, cols = factors(tiles)
        ref = self.ruler.at[pl.ds(0, rows * 16), pl.ds(0, cols * 128)]
        pltpu.make_async_copy(ref, ref, sem).wait()

    def wait(self, key):
        index, tiles = self.keys[key]
        self.wait_tiles(tiles, self.recv_sems.at[index])

    def wait_sent(self):
        for i, (size, count) in enumerate(self.sizes):
            self.wait_tiles(size * count, self.send_sems.at[i])

    def load(self, src, dst):
        i = self.used_local
        self.used_local += 1
        copy = pltpu.make_async_copy(src, dst, self.local_sems.at[i])
        copy.start()
        return copy


def kernel(
    a_in, w_in, r_in, gain, p_in, s_in, sr_in, ws_in, out,
    a_v, w_v, c_v, ra, rb, ry, ry4, r_v, hg_v, p_v, ws_t, ws_v, s_v, st_v, sr_t, sr_v, t_v, so_v, g_v,
    iv_v, grad, ga1, gb1, ga2, gb2, ra2, rb2, fin, o_r,
    send_sems, recv_sems, local_sems,
):
    net = Net(send_sems, recv_sems, local_sems, w_in)
    x, y, z, c = net.x, net.y, net.z, net.c
    other_c = 1 - c
    yh, yl = lax.div(y, 2), lax.rem(y, 2)
    other_yh = 1 - yh
    my_cols = pl.ds(pl.multiple_of(z * 512 + c * 256, 256), 256)
    mine = pl.ds(pl.multiple_of(c * 256, 256), 256)
    theirs = pl.ds(pl.multiple_of(other_c * 256, 256), 256)

    def slab(zv):
        return pl.ds(pl.multiple_of(zv * 512, 512), 512)

    partners = [{axis: 2} for axis in "xyz"] + [dict(z=by, c=1) for by in (2, 1, 3)] + [{axis: by} for axis in "xyz" for by in (1, 3)] + [dict(c=1)]
    barrier = pltpu.get_barrier_semaphore()
    for where in partners:
        pl.semaphore_signal(barrier, inc=1, device_id=net.at(**where), device_id_type=MESH)

    load_a = net.load(a_in, a_v)
    w_loads = {}

    def load_w(n):
        if n < len(W_ORDER):
            k = W_ORDER[n]
            cols = pl.ds(STARTS[k], WIDTHS[k])
            w_loads[n] = net.load(w_in.at[:, cols], w_v.at[n % 2, :, pl.ds(0, WIDTHS[k])])

    load_w(0)

    def ahead(by):
        return step(x, by)

    def products(k):
        n = W_ORDER.index(k)
        w_loads[n].wait()

        @pl.loop(0, WIDTHS[k] // 256)
        def _(j):
            cols = pl.ds(pl.multiple_of(j * 256, 256), 256)
            res = jnp.dot(a_v[...].reshape(1280, 1024), w_v[n % 2, :, cols], preferred_element_type=F32)
            c_v[k, :, :, :, cols] = res.astype(BF16).reshape(4, 2, 160, 256)

        load_w(n + 2)

    low, high = pl.ds(0, 80), pl.ds(80, 80)

    def block(ref, *index, rows=pl.ds(0, 160)):
        return ref.at[(*index, rows, pl.ds(0, WIDTHS[index[0]]))]

    def read(ref, *index, rows=pl.ds(0, 160)):
        return block(ref, *index, rows=rows)[...].astype(F32)

    def write(value, ref, *index, rows=pl.ds(0, 160)):
        block(ref, *index, rows=rows)[...] = value.astype(BF16)

    def x_far(k):
        net.send(("far", k), block(c_v, k, ahead(2), 0), block(ra, k, 0), x=1)
        net.send(("far", k), block(c_v, k, ahead(2), 1), block(ra, k, 1), x=3)

    def x_direct(k):
        net.send(("near", k), block(c_v, k, ahead(1), 1), block(rb, k, 0, 1), x=1)
        net.send(("near", k), block(c_v, k, ahead(3), 0), block(rb, k, 1, 0), x=3)

    def x_relay(k):
        net.wait(("far", k))
        for way, rel, by in ((0, 1, 1), (1, 3, 3)):
            to = ahead(rel)
            write(read(c_v, k, to, way) + read(ra, k, way), c_v, k, to, way)
            net.send(("near", k), block(c_v, k, to, way), block(rb, k, way, way), x=by)

    def x_total(k, h):
        return read(c_v, k, x, h) + read(rb, k, 0, h) + read(rb, k, 1, h)

    def x_sum(k):
        net.wait(("near", k))
        write(x_total(k, other_yh), c_v, k, x, other_yh)
        net.send(("y", k), block(c_v, k, x, other_yh), block(ry, k), y=2)

    squares = []

    def hidden_out(k, attended):
        cols = pl.ds(STARTS[k], WIDTHS[k])
        hidden = r_v[:, cols].astype(F32) + attended
        squares.append(jnp.sum(hidden * hidden, axis=-1, keepdims=True))
        write(hidden * gain[:, cols], hg_v, k, z, c)
        ref = block(hg_v, k, z, c)
        for by in (1, 3):
            net.send(("hg", k), ref, ref, z=by)
        net.send(("pair", k), ref, ref, c=1)

    def y_sum(k):
        net.wait(("y", k))
        hidden_out(k, x_total(k, yh) + read(ry, k))

    def y_first_send(k, rel):
        ref = ry4.at[Y_FIRST.index(k), rel, :, pl.ds(0, WIDTHS[k])]
        net.send(("y", k, rel), block(c_v, k, ahead(rel), other_yh), ref, y=2)

    def y_first_add(k, rel):
        net.wait(("y", k, rel))
        ref = ry4.at[Y_FIRST.index(k), rel, :, pl.ds(0, WIDTHS[k])]
        write(read(c_v, k, ahead(rel), yh) + ref[...].astype(F32), c_v, k, ahead(rel), yh)

    def y_first_far(k):
        y_first_add(k, 2)
        net.send(("far", k), block(c_v, k, ahead(2), yh, rows=low), block(ra, k, 0, rows=low), x=1)
        net.send(("far", k), block(c_v, k, ahead(2), yh, rows=high), block(ra, k, 1, rows=high), x=3)

    def y_first_direct(k):
        y_first_add(k, 1)
        net.send(("near", k), block(c_v, k, ahead(1), yh, rows=high), block(rb, k, 0, 0, rows=high), x=1)
        y_first_add(k, 3)
        net.send(("near", k), block(c_v, k, ahead(3), yh, rows=low), block(rb, k, 1, 0, rows=low), x=3)

    def y_first_relay(k):
        net.wait(("far", k))
        for way, rel, by, rows in ((0, 1, 1, low), (1, 3, 3, high)):
            to = ahead(rel)
            write(read(c_v, k, to, yh, rows=rows) + read(ra, k, way, rows=rows), c_v, k, to, yh, rows=rows)
            net.send(("near", k), block(c_v, k, to, yh, rows=rows), block(rb, k, way, 0, rows=rows), x=by)

    def y_first_out(k):
        y_first_add(k, 0)
        net.wait(("near", k))
        hidden_out(k, read(c_v, k, x, yh) + read(rb, k, 0, 0) + read(rb, k, 1, 0))

    def hg_on(k):
        net.wait(("hg", k))
        for by, rows in ((1, low), (3, high)):
            source = step(z, 4 - by)
            ref = block(hg_v, k, source, c, rows=rows)
            net.send(("on", k), ref, ref, z=by)
        for by in (1, 3):
            ref = block(hg_v, k, step(z, 4 - by), c)
            net.send(("pair", k), ref, ref, c=1)

    def hg_end(k):
        net.wait(("on", k))
        ref = block(hg_v, k, step(z, 2), c)
        net.send(("pair", k), ref, ref, c=1)

    def hg_dot(k):
        net.wait(("pair", k))
        start, width = STARTS[k], WIDTHS[k]
        shard = start // 512
        halves = p_v[shard // 2, shard % 2]
        if width == 256:
            halves = halves[start % 512 // 256]
        t_v[...] += jnp.dot(
            hg_v[k, :, :, :, :width].reshape(1280, width),
            halves.reshape(width, 256),
            preferred_element_type=F32,
        ).reshape(4, 320, 256)

    begins = ((1, pl.ds(0, 128)), (3, pl.ds(128, 128)))

    def p_x():
        for by in (1, 3):
            net.send("p_x", p_in.at[yl, :, my_cols], p_v.at[x, yh, yl], x=by)

    def p_x_on():
        net.wait("p_x")
        for by, cols in begins:
            ref = p_v.at[step(x, 4 - by), yh, yl, :, cols]
            net.send("p_x_on", ref, ref, x=by)

    def p_at(yv, cols):
        return p_v.at[:, lax.div(yv, 2), lax.rem(yv, 2), :, cols]

    def p_ring():
        load_p.wait()
        net.wait("p_x_on")
        ref = p_at(y, pl.ds(0, 256))
        for by in (1, 3):
            net.send("p_ring", ref, ref, y=by)

    def p_on():
        net.wait("p_ring")
        for by, cols in begins:
            ref = p_at(step(y, 4 - by), cols)
            net.send("p_on", ref, ref, y=by)

    def ws_z():
        for by in (1, 3, 2):
            net.send("ws_z", ws_in.at[:, slab(step(z, by))], ws_t.at[z], z=by)

    def w_pair():
        load_ws.wait()
        net.wait("ws_z")
        net.send("w_pair", ws_t.at[:, :, theirs], ws_v.at[yl, :, c, x, yh], c=1)
        return net.load(ws_t.at[:, :, mine], ws_v.at[yl, :, c, x, yh])

    def w_x(copy):
        copy.wait()
        net.wait("w_pair")
        ref = ws_v.at[yl, :, :, x, yh]
        for by in (1, 3):
            net.send("w_x", ref, ref, x=by)

    def w_x_on():
        net.wait("w_x")
        for by, cols in begins:
            ref = ws_v.at[yl, :, :, step(x, 4 - by), yh, :, cols]
            net.send("w_x_on", ref, ref, x=by)

    def ws_at(yv, cols):
        return ws_v.at[lax.rem(yv, 2), :, :, :, lax.div(yv, 2), :, cols]

    def ws_ring():
        net.wait("w_x_on")
        ref = ws_at(y, pl.ds(0, 256))
        for by in (1, 3):
            net.send("ws_ring", ref, ref, y=by)

    def ws_on():
        net.wait("ws_ring")
        for by, cols in begins:
            ref = ws_at(step(y, 4 - by), cols)
            net.send("ws_on", ref, ref, y=by)

    def s_ring():
        for by in (1, 3):
            net.send("s_ring", s_in, s_v.at[z, c], z=by)
        net.send("s_pair", s_in, s_v.at[z, c], c=1)

    def s_on():
        net.wait("s_ring")
        for by, rows in ((1, low), (3, high)):
            ref = s_v.at[step(z, 4 - by), c, rows]
            net.send("s_on", ref, ref, z=by)
        for by in (1, 3):
            ref = s_v.at[step(z, 4 - by), c]
            net.send("s_pair", ref, ref, c=1)

    def s_end():
        net.wait("s_on")
        ref = s_v.at[step(z, 2), c]
        net.send("s_pair", ref, ref, c=1)

    def sr_z():
        for by in (1, 3, 2):
            net.send("sr_z", sr_in.at[:, slab(step(z, by))], sr_t.at[z], z=by)

    def sr_end():
        load_sr.wait()
        net.wait("sr_z")
        net.send("sr_pair", sr_t.at[:, :, theirs], sr_v.at[:, c], c=1)
        return net.load(sr_t.at[:, :, mine], sr_v.at[:, c])

    def transpose():
        load_s.wait()
        net.wait("s_pair")

        @pl.loop(0, 8)
        def _(j):
            cols = pl.ds(pl.multiple_of(j * 256, 256), 256)
            st_v[cols] = s_v[:, :, :, cols].reshape(1280, 256).T

    def student(copy):
        copy.wait()
        net.wait("sr_pair")
        net.wait("ws_on")

        @pl.loop(0, 4)
        def _(i):
            so_v[i] = sr_v[i].reshape(320, 256).astype(F32) + jnp.dot(
                s_v[i].reshape(320, 2048), ws_v[...].reshape(2048, 256), preferred_element_type=F32
            )


    pl.semaphore_wait(barrier, len(partners))
    p_x()
    ws_z()
    s_ring()
    load_a.wait()
    load_w(1)
    load_p = net.load(p_in.at[yl, :, my_cols], p_v.at[x, yh, yl])
    load_ws = net.load(ws_in.at[:, slab(z)], ws_t.at[z])
    load_sr = net.load(sr_in.at[:, slab(z)], sr_t.at[z])
    load_s = net.load(s_in, s_v.at[z, c])
    load_r = net.load(r_in, r_v)
    t_v[...] = jnp.zeros_like(t_v)
    products(5)
    x_direct(5)
    products(3)
    products(1)
    x_far(5)
    p_x_on()
    x_far(1)
    y_first_send(3, 1)
    y_first_send(3, 2)
    products(6)
    products(0)
    products(7)
    x_far(0)
    y_first_send(3, 0)
    y_first_send(3, 3)
    y_first_send(7, 1)
    x_direct(1)
    y_first_send(7, 2)
    x_relay(1)
    products(2)
    sr_z()
    y_first_far(3)
    x_relay(5)
    y_first_direct(3)
    p_ring()
    x_sum(5)
    x_far(6)
    y_first_send(7, 3)
    s_on()
    w_copy = w_pair()
    y_first_relay(3)
    y_first_far(7)
    x_direct(0)
    x_sum(1)
    load_r.wait()
    y_first_out(3)
    x_relay(0)
    w_x(w_copy)
    x_far(2)
    hg_on(3)
    x_relay(6)
    y_sum(1)
    products(4)
    y_first_direct(7)
    y_first_send(7, 0)
    p_on()
    y_sum(5)
    x_relay(2)
    x_sum(0)
    x_direct(2)
    y_first_relay(7)
    hg_on(1)
    hg_end(1)
    hg_on(5)
    y_first_out(7)
    w_x_on()
    x_direct(6)
    x_sum(2)
    hg_end(5)
    y_sum(0)
    x_far(4)
    x_sum(6)
    hg_on(7)
    x_direct(4)
    hg_end(3)
    net.wait("p_on")
    hg_dot(1)
    y_sum(2)
    s_end()
    ws_ring()
    x_relay(4)
    hg_on(0)
    y_sum(6)
    x_sum(4)
    sr_copy = sr_end()
    hg_end(0)
    hg_dot(5)
    transpose()
    hg_end(7)
    hg_on(2)
    hg_on(6)
    hg_dot(3)
    y_sum(4)
    hg_end(2)
    ws_on()
    hg_dot(2)
    hg_end(6)
    hg_dot(7)
    hg_dot(0)
    inverse = lax.rsqrt(sum(squares) * (1.0 / 4096.0) + 1e-05)
    iv_v[z, c, :, 0:160] = jnp.broadcast_to(inverse, (160, 128)).T[:8]
    for by in (1, 3, 2):
        net.send("scale", iv_v.at[z, c], iv_v.at[z, c], z=by)
    hg_on(4)
    student(sr_copy)
    hg_end(4)
    hg_dot(6)
    net.wait("scale")
    net.send("scale_pair", iv_v.at[:, c], iv_v.at[:, c], c=1)
    hg_dot(4)
    net.wait("scale_pair")
    for i in range(4):
        for core in range(2):
            scale = iv_v[i, core, :, 0:160].T[:, 0:1]
            rows = pl.ds(core * 160, 160)
            g_v[i, rows] = (128.0 / 20480.0 * (so_v[i, rows] - scale * t_v[i, rows])).astype(BF16)

    left, right = pl.ds(0, 128), pl.ds(128, 128)
    for half, near in ((1 - yl, (1, 3)), (yl, (2,))):

        @pl.loop(0, 2)
        def _(i):
            rows = pl.ds(pl.multiple_of(half * 1024 + i * 512, 512), 512)
            res = jnp.dot(st_v[rows], g_v[...].reshape(1280, 256), preferred_element_type=F32)
            grad[half, pl.ds(i * 2, 2)] = res.astype(BF16).reshape(2, 2, 4, 2, 16, 256)

        for by in near:
            ref = grad.at[half, :, :, :, lax.div(step(y, by), 2), :, right]
            net.send("y_1", ref, gb1.at[by - 1], y=by)
        for by in (2, 1, 3):
            net.send("x_1", grad.at[half, :, :, step(x, by), :, :, left], ga1.at[by - 1, half], x=by)

    def four(own, others):
        return own.astype(F32) + others[0].astype(F32) + others[1].astype(F32) + others[2].astype(F32)

    net.wait("x_1")
    ga2[...] = four(grad[:, :, :, x, :, :, left], ga1).astype(BF16)
    for by in (2, 1, 3):
        to = step(y, by)
        net.send("y_2", ga2.at[lax.rem(to, 2), :, :, lax.div(to, 2)], ra2.at[by - 1], y=by)
    net.wait("y_1")
    gb2[...] = four(grad[yl, :, :, :, yh, :, right], gb1).astype(BF16)
    for by in (2, 1, 3):
        net.send("x_2", gb2.at[:, :, step(x, by)], rb2.at[by - 1], x=by)
    net.wait("y_2")
    fin[:, :, :, left] = four(ga2[yl, :, :, yh], ra2)
    net.wait("x_2")
    fin[:, :, :, right] = four(gb2[:, :, x], rb2)

    for by, core in ((2, 1), (2, 0), (1, 1), (3, 1), (1, 0), (3, 0), (0, 1)):
        ref = fin.at[step(z, by), lax.rem(c + core, 2)]
        net.send("rows", ref, o_r.at[z, c], z=by, c=core)
    o_r[z, c] = fin[z, c]
    net.wait("rows")
    for i in range(4):
        for core in range(2):
            out[:, pl.ds(i * 512 + core * 256, 256)] = o_r[i, core]

    net.wait_sent()


def per_device(a, w, resid, gain, projector, s, s_resid, ws):
    anywhere = pl.BlockSpec(memory_space=pl.ANY)
    vmem = pl.BlockSpec(memory_space=pltpu.VMEM)
    chunks = len(WIDTHS)
    return pl.pallas_call(
        kernel,
        out_shape=jax.ShapeDtypeStruct((16, 2048), F32),
        in_specs=[anywhere, anywhere, anywhere, vmem, anywhere, anywhere, anywhere, anywhere],
        out_specs=vmem,
        scratch_shapes=[
            pltpu.VMEM((4, 320, 1024), BF16),
            pltpu.VMEM((2, 1024, WIDE), BF16),
            pltpu.VMEM((chunks, 4, 2, 160, WIDE), BF16),
            pltpu.VMEM((chunks, 2, 160, WIDE), BF16),
            pltpu.VMEM((chunks, 2, 2, 160, WIDE), BF16),
            pltpu.VMEM((chunks, 160, WIDE), BF16),
            pltpu.VMEM((len(Y_FIRST), 4, 160, WIDE), BF16),
            pltpu.VMEM((160, 4096), BF16),
            pltpu.VMEM((chunks, 4, 2, 160, WIDE), BF16),
            pltpu.VMEM((4, 2, 2, 256, 256), BF16),
            pltpu.VMEM((4, 16, 512), BF16),
            pltpu.VMEM((2, 4, 2, 4, 2, 16, 256), BF16),
            pltpu.VMEM((4, 2, 160, 2048), BF16),
            pltpu.VMEM((2048, 1280), BF16),
            pltpu.VMEM((4, 160, 512), BF16),
            pltpu.VMEM((4, 2, 160, 256), BF16),
            pltpu.VMEM((4, 320, 256), F32),
            pltpu.VMEM((4, 320, 256), F32),
            pltpu.VMEM((4, 320, 256), BF16),
            pltpu.VMEM((4, 2, 8, 256), F32),
            pltpu.VMEM((2, 4, 2, 4, 2, 16, 256), BF16),
            pltpu.VMEM((3, 2, 4, 2, 2, 16, 128), BF16),
            pltpu.VMEM((3, 4, 2, 4, 16, 128), BF16),
            pltpu.VMEM((2, 4, 2, 2, 16, 128), BF16),
            pltpu.VMEM((4, 2, 4, 16, 128), BF16),
            pltpu.VMEM((3, 4, 2, 16, 128), BF16),
            pltpu.VMEM((3, 4, 2, 16, 128), BF16),
            pltpu.VMEM((4, 2, 16, 256), F32),
            pltpu.VMEM((4, 2, 16, 256), F32),
            pltpu.SemaphoreType.DMA((N_SEND,)),
            pltpu.SemaphoreType.DMA((N_RECV,)),
            pltpu.SemaphoreType.DMA((N_LOCAL,)),
        ],
        compiler_params=pltpu.CompilerParams(
            collective_id=0, has_side_effects=True, vmem_limit_bytes=62 * 2**20
        ),
        cost_estimate=pl.CostEstimate(flops=16 * 10**9, bytes_accessed=16 * 10**6, transcendentals=160),
    )(
        a.reshape(4, 320, 1024),
        w,
        resid,
        gain.reshape(1, 4096),
        projector.reshape(2, 256, 2048),
        s,
        s_resid,
        ws,
    )


def solution(mesh):
    return jax.shard_map(
        per_device,
        mesh=mesh,
        in_specs=(
            P("dp", "tensor"),
            P("tensor", None),
            P(("dp", "tensor"), None),
            P(),
            P("tensor", None),
            P(("dp", "tensor"), None),
            P(("dp", "tensor"), None),
            P(("dp", "tensor"), None),
        ),
        out_specs=P(("dp", "tensor"), None),
        check_vma=False,
    )
```
